512 devices in a mesh: src: 16 (over z, y_hi), tgt: 32 (over x, y_lo, core).
Axes of the slice: x: 4, y: 8 (y_hi: 2, y_lo: 4; y = y_hi * 4 + y_lo), z: 8, core: 2. Of those that a mesh axis runs over, the one named last changes fastest.
Arguments:
- hidden_in: bfloat16 [8192, 4096], P('tgt', 'src'), may hold values from -6 to 6
- norm_gain: bfloat16 [4096], replicated, may hold values from 0.25 to 1.75
- w_query: bfloat16 [4096, 4096], P(None, 'src'), may hold values from -0.09375 to 0.09375
- keys_cache: bfloat16 [4096, 4096], P('tgt', 'src')
- values_cache: bfloat16 [4096, 4096], P('tgt', 'src'), may hold values from -6 to 6
- lengths: int32 [16], replicated, may hold values from 1 to 256, 2560 in all
- w_output: bfloat16 [4096, 4096], P(None, 'src'), may hold values from -1.5 to 1.5
Outputs:
- hidden_out: float32 [8192, 4096], P('tgt', 'src')
The draws below stay inside these ranges and needn't reach their ends.
Inputs may be any that keep to these rules, and one draw needn't show every extreme that they name: `lengths`: the source holds 16 responses of 256 positions each, response r at positions r * 256 onward; one response is full in every draw.
All inputs are finite; a program needn't handle non-finite values.
Results may differ from the reference program's by a relative error of at most 0.035.
Values may be sent and summed in bfloat16 or wider, within the bound.
A program may use at most 128 MiB of HBM per device.

```python
import math
import jax
import jax.numpy as jnp
import numpy as np
from jax import lax

D = 4096
HEADS = 64
HD = 64
RESP = 16
INNER = 4096
TOKENS = 8192
SRC_LEN = 4096
SLOT = 256


def draw_keys_cache(key, part):
    key = jax.random.fold_in(key, 11)
    first = jax.random.fold_in(key, 0)
    base = jax.random.normal(first, (SRC_LEN, INNER), jnp.float32)
    return base.astype(jnp.bfloat16)


def shard_levels(key, shape, cuts, low, top_value):
    gain = 1.0
    for position, blocks in cuts:
        steps = jax.random.uniform(jax.random.fold_in(jax.random.fold_in(key, 6), position), (blocks,), jnp.float32, low / len(cuts), top_value / len(cuts))
        gain = gain * jnp.repeat(jnp.exp(steps), shape[position] // blocks).reshape((-1,) + (1,) * (len(shape) - 1 - position))
    return gain


def length_profile(number_of, total, most, lean):
    portions = [(1 << 20) // math.isqrt(grade ** lean) + 1 for grade in range(2, number_of + 1)]
    rest, given = total - most - (number_of - 1), [1] * (number_of - 1)
    while rest > 0:
        candidates = [i for i in range(number_of - 1) if given[i] < most]
        mass, budget = sum([portions[i] for i in candidates]), rest
        for i in candidates:
            addition = min(most - given[i], max(1, budget * portions[i] // mass), rest)
            given[i] = given[i] + addition
            rest = rest - addition
    return np.array([most] + given)


def ragged(own_key, number_of, total, reach, skew):
    if number_of == 2:
        one = jax.random.randint(own_key, (), max(1, total - reach), min(reach, total - 1) + 1)
        return jnp.stack([one, total - one])
    sizes = jnp.asarray(length_profile(number_of, total, reach, skew), jnp.int32)
    couples = (number_of - 1) // 2
    donor, sink = sizes[1:1 + 2 * couples:2], sizes[2:2 + 2 * couples:2]
    margin = jnp.minimum(donor - 1, reach - sink)
    moved = jax.random.randint(jax.random.fold_in(own_key, 1), (couples,), 0, 1 << 20) % (margin + 1)
    sizes = sizes.at[1:1 + 2 * couples:2].set(donor - moved).at[2:2 + 2 * couples:2].set(sink + moved)
    return sizes[jax.random.permutation(jax.random.fold_in(own_key, 2), number_of)]


def noise(own_key, dims, scale, bound, shards=(), kind=jnp.bfloat16):
    drawn = scale * jax.random.normal(own_key, dims, jnp.float32)
    if shards:
        drawn = drawn * shard_levels(own_key, dims, shards, -0.22, 0.18)
    return jnp.clip(drawn, -bound, bound).astype(kind)


def setup_inputs(seed: int = 0) -> dict:
    keys = jax.random.split(jax.random.key(seed), 8)
    hidden_in = noise(keys[0], (TOKENS, D), 1.0, 6.0, ((0, 32), (1, 16)))
    norm_gain = jnp.clip(1.0 + 0.15 * jax.random.normal(keys[1], (D,), jnp.float32), 0.25, 1.75).astype(jnp.bfloat16)
    w_query = noise(keys[2], (D, INNER), D ** -0.5, 0.09375, ((1, 16),))
    keys_cache = draw_keys_cache(jax.random.fold_in(keys[7], 71), 0)
    values_cache = noise(keys[4], (SRC_LEN, INNER), 1.0, 6.0, ((0, 32), (1, 16)))
    lengths = ragged(keys[5], RESP, RESP * SLOT * 5 // 8, SLOT, 1).astype(jnp.int32)
    w_output = noise(keys[6], (INNER, D), (max(INNER // 256, 1)) ** -0.5, 1.5, ((1, 16),))
    return {"hidden_in": hidden_in, "norm_gain": norm_gain, "w_query": w_query, "keys_cache": keys_cache, "values_cache": values_cache, "lengths": lengths, "w_output": w_output}


def reference(hidden_in, norm_gain, w_query, keys_cache, values_cache, lengths, w_output):
    source = hidden_in.astype(jnp.float32)
    spread = lax.optimization_barrier(jnp.mean(source * source, axis=-1, keepdims=True))
    normed = (source * lax.rsqrt(spread + 1e-06) * norm_gain.astype(jnp.float32)).astype(jnp.bfloat16)
    queries = jnp.dot(normed, w_query, preferred_element_type=jnp.float32).astype(jnp.bfloat16)
    positions = jnp.arange(SRC_LEN, dtype=jnp.int32)
    allowed = positions % SLOT < lengths[positions // SLOT]
    q_heads = queries.astype(jnp.float32).reshape(TOKENS, HEADS, HD).transpose(1, 0, 2)
    k_heads = keys_cache.astype(jnp.float32).reshape(SRC_LEN, HEADS, HD).transpose(1, 0, 2)
    v_heads = values_cache.astype(jnp.float32).reshape(SRC_LEN, HEADS, HD).transpose(1, 0, 2)

    def one_head(operands):
        q_one, k_one, v_one = operands
        scores = jnp.dot(q_one, k_one.T, precision=lax.Precision.HIGHEST) * HD ** (-0.5)
        scores = jnp.where(allowed[None, :], scores, -1e+30)
        top = lax.optimization_barrier(jnp.max(scores, axis=1, keepdims=True))
        expd = jnp.where(allowed[None, :], jnp.exp(scores - top), 0.0)
        denom = lax.optimization_barrier(jnp.sum(expd, axis=1, keepdims=True))
        rounded = lax.optimization_barrier(expd.astype(jnp.bfloat16))
        numer = jnp.dot(rounded.astype(jnp.float32), v_one, precision=lax.Precision.HIGHEST)
        return numer / denom
    attended = lax.map(one_head, (q_heads, k_heads, v_heads))
    attended = attended.transpose(1, 0, 2).reshape(TOKENS, INNER).astype(jnp.bfloat16)
    branch = jnp.dot(attended, w_output, preferred_element_type=jnp.float32)
    return source + branch
```

```python
import functools

import jax
import jax.numpy as jnp
from jax import lax
from jax.experimental import pallas as pl
from jax.experimental.pallas import tpu as pltpu
from jax.sharding import PartitionSpec as P

MESH = pl.DeviceIdType.MESH
HD = 64
NZ, NX, NYL = 8, 4, 4
SRC, TGT = 16, 32
TOK, FEAT, POS, WIDE = 256, 256, 128, 4096
PAIR = 128
BLK = 512
NB = WIDE // BLK
SCALE = HD ** -0.5 * 1.4426950408889634
F32, BF16 = jnp.float32, jnp.bfloat16
NT = (((1,), (1,)), ((), ()))


def kernel(
    hid_hbm, gain_ref, wq_hbm, keys_hbm, vals_hbm, len_ref, wo_hbm, out_ref,
    hbuf, kv, kc, vp, wq, wo, abuf, sbuf, mbuf, obuf, qacc, ssq, qm, krow,
    loc_sem, h_send, h_recv, a_send, a_recv, kv_send, kv_recv, kk_recv, vv_recv,
):
    src = lax.axis_index("src")
    tgt = lax.axis_index("tgt")
    z, yh = src // 2, src % 2
    x, yl, core = tgt // 8, (tgt // 2) % 4, tgt % 2
    partner = z * 2 + (1 - yh)
    z_right = ((z + 1) % NZ) * 2 + yh
    z_left = ((z + NZ - 1) % NZ) * 2 + yh
    sib = x * 8 + yl * 2 + (1 - core)

    def at_tgt(xx, yy):
        return (xx % NX) * 8 + (yy % NYL) * 2 + core

    x_right, x_left = at_tgt(x + 1, yl), at_tgt(x + NX - 1, yl)

    loads = [
        pltpu.make_async_copy(hid_hbm, hbuf.at[src], loc_sem.at[0]),
        pltpu.make_async_copy(keys_hbm, kv.at[tgt, 0], loc_sem.at[1]),
        pltpu.make_async_copy(vals_hbm, kv.at[tgt, 1], loc_sem.at[2]),
        pltpu.make_async_copy(wq_hbm, wq, loc_sem.at[3]),
        pltpu.make_async_copy(wo_hbm, wo, loc_sem.at[4]),
    ]
    for c in loads:
        c.start()

    barrier = pltpu.get_barrier_semaphore()
    friends = [
        (partner, tgt), (z_right, tgt), (z_left, tgt),
        (src, x_right), (src, x_left), (src, sib),
        (src, at_tgt(x, yl + 1)), (src, at_tgt(x, yl + 2)), (src, at_tgt(x, yl + 3)),
    ]
    for f in friends:
        pl.semaphore_signal(barrier, inc=1, device_id=f, device_id_type=MESH)

    qacc[...] = jnp.zeros_like(qacc)
    ssq[...] = jnp.zeros_like(ssq)
    for c in loads[:3]:
        c.wait()
    pl.semaphore_wait(barrier, len(friends))

    pending = []

    def send(ref, ssem, rsem, dev):
        c = pltpu.make_async_remote_copy(
            src_ref=ref, dst_ref=ref, send_sem=ssem, recv_sem=rsem,
            device_id=dev, device_id_type=MESH,
        )
        c.start()
        pending.append(c)

    def arrived(ref, rsem):
        pltpu.make_async_remote_copy(
            src_ref=ref, dst_ref=ref, send_sem=rsem, recv_sem=rsem,
            device_id=(src, sib), device_id_type=MESH,
        ).wait_recv()

    def owner_of(col, dist, way):
        zz = (z - dist + NZ) % NZ if way == "R" else (z + dist) % NZ
        return zz * 2 + (yh if col == 0 else 1 - yh)

    class Ring:
        def __init__(self, slot, ssem, rsem):
            self.slot, self.ssem, self.rsem, self.count = slot, ssem, rsem, 0

        def push(self, owner, half, dev):
            send(self.slot(owner, half), self.ssem.at[self.count], self.rsem.at[owner * 2 + half], dev)
            self.count += 1

        def own(self, half):
            self.push(src, half, (z_right, tgt))
            self.push(src, half, (z_left, tgt))
            self.push(src, half, (partner, tgt))

        def take(self, col, dist, way, half):
            owner = owner_of(col, dist, way)
            arrived(self.slot(owner, half), self.rsem.at[owner * 2 + half])
            last = {("R", 0): 3, ("R", 1): 2, ("L", 0): 2, ("L", 1): 3}[(way, col)]
            if dist <= last:
                self.push(owner, half, (z_right if way == "R" else z_left, tgt))
            return owner

        def both(self, col, dist, half):
            ways = "RL" if dist < 4 else ("R" if col == 0 else "L")
            return [self.take(col, dist, way, half) for way in ways]

        def cross(self, half):
            arrived(self.slot(partner, half), self.rsem.at[partner * 2 + half])
            self.push(partner, half, (z_right, tgt))
            self.push(partner, half, (z_left, tgt))

    hid = Ring(lambda o, h: hbuf.at[o, pl.ds(h * 128, 128)], h_send, h_recv)
    att = Ring(lambda o, h: abuf.at[o, h], a_send, a_recv)
    kv_count = [0]

    def kv_push(ref, rsem, dev):
        send(ref, kv_send.at[kv_count[0]], rsem, dev)
        kv_count[0] += 1

    def to_sibling(s):
        kv_push(kv.at[s], kv_recv.at[s], (src, sib))

    def q_part(owner):
        h = hbuf[owner].astype(F32)
        sq = h * h
        ssq[...] += sq[:, :128] + sq[:, 128:]
        hg = (h * gain_ref[owner]).astype(BF16)
        w = wq[pl.ds(pl.multiple_of(owner * FEAT, FEAT), FEAT), :]
        qacc[...] += jnp.dot(hg, w, preferred_element_type=F32)

    def prep(s):
        limit = len_ref[s // 2] - (s % 2) * POS
        rows = lax.broadcasted_iota(jnp.int32, (POS, FEAT), 0)
        at = pl.ds(pl.multiple_of(s * POS, POS), POS)
        k = kv[s, 0].astype(F32)
        kc[at, :] = jnp.where(rows < limit, k, krow[0:1, :]).astype(BF16)
        v = kv[s, 1].astype(F32)
        ok = rows[:, :PAIR] < limit
        low = lax.broadcasted_iota(jnp.int32, (POS, PAIR), 1) < HD
        for p in range(2):
            vv = v[:, p * PAIR:(p + 1) * PAIR]
            vp[2 * p, at, :] = jnp.where(ok, jnp.where(low, vv, 1.0), 0.0).astype(BF16)
            vp[2 * p + 1, at, :] = jnp.where(ok, jnp.where(low, 1.0, vv), 0.0).astype(BF16)

    for half in range(2):
        hid.own(half)
    kv_push(kv.at[tgt], kv_recv.at[tgt], (src, x_right))
    kv_push(kv.at[tgt], kv_recv.at[tgt], (src, x_left))
    to_sibling(tgt)
    for k in (1, 3, 2):
        kv_push(kv.at[tgt], kv_recv.at[tgt], (src, at_tgt(x, yl + k)))

    loads[3].wait()
    q_part(src)

    def y_take(k):
        s = at_tgt(x, yl + k)
        arrived(kv.at[s], kv_recv.at[s])
        kv_push(kv.at[s], kv_recv.at[s], (src, x_right))
        kv_push(kv.at[s], kv_recv.at[s], (src, x_left))
        to_sibling(s)
        return s

    def x_take(k):
        s_left, s_right = at_tgt(x + NX - 1, yl + k), at_tgt(x + 1, yl + k)
        arrived(kv.at[s_left], kv_recv.at[s_left])
        kv_push(kv.at[s_left, 0], kk_recv.at[s_left], (src, x_right))
        arrived(kv.at[s_right], kv_recv.at[s_right])
        kv_push(kv.at[s_right, 1], vv_recv.at[s_right], (src, x_left))
        to_sibling(s_left)
        to_sibling(s_right)
        return s_left, s_right

    def far_take(k):
        s = at_tgt(x + 2, yl + k)
        arrived(kv.at[s, 0], kk_recv.at[s])
        arrived(kv.at[s, 1], vv_recv.at[s])
        to_sibling(s)
        return s

    def sib_of(s):
        return s + 1 - 2 * core

    def sib_take(s):
        o = sib_of(s)
        arrived(kv.at[o], kv_recv.at[o])
        return o

    hid.both(0, 1, 0)
    for o in hid.both(0, 1, 1):
        q_part(o)
    s_l0, s_r0 = x_take(0)
    o = sib_take(tgt)
    krow[...] = jnp.broadcast_to(
        kv[x * 8 + yl * 2, 0, 0:16, :].astype(F32)[0:1, :], krow.shape
    )
    prep(tgt)
    prep(o)
    hid.both(0, 2, 0)
    s_y1 = y_take(1)
    prep(s_l0)
    prep(s_r0)
    for o in hid.both(0, 2, 1):
        q_part(o)
    s_f0 = far_take(0)
    s_y3 = y_take(3)
    prep(s_y1)
    hid.cross(0)
    hid.cross(1)
    hid.both(0, 3, 0)
    q_part(partner)
    s_y2 = y_take(2)
    prep(s_f0)
    prep(s_y3)
    for o in hid.both(0, 3, 1):
        q_part(o)
    s_l1, s_r1 = x_take(1)
    prep(s_y2)
    prep(sib_take(s_l0))
    prep(sib_take(s_r0))
    hid.both(0, 4, 0)
    hid.both(1, 1, 0)
    prep(sib_take(s_y1))
    prep(sib_take(s_f0))
    for o in hid.both(0, 4, 1) + hid.both(1, 1, 1):
        q_part(o)
    s_f1 = far_take(1)
    s_l3, s_r3 = x_take(3)
    prep(s_l1)
    prep(s_r1)
    prep(sib_take(s_y3))
    hid.both(1, 2, 0)
    prep(s_f1)
    prep(s_l3)
    prep(s_r3)
    prep(sib_take(s_y2))
    for o in hid.both(1, 2, 1):
        q_part(o)
    s_f3 = far_take(3)
    prep(sib_take(s_l1))
    prep(sib_take(s_r1))
    s_l2, s_r2 = x_take(2)
    prep(s_f3)
    prep(sib_take(s_f1))
    hid.both(1, 3, 0)
    prep(s_l2)
    prep(s_r2)
    prep(sib_take(s_l3))
    prep(sib_take(s_r3))
    for o in hid.both(1, 3, 1):
        q_part(o)
    hid.both(1, 4, 0)
    s_f2 = far_take(2)
    prep(s_f2)
    prep(sib_take(s_f3))
    prep(sib_take(s_l2))
    prep(sib_take(s_r2))
    for o in hid.both(1, 4, 1):
        q_part(o)
    prep(sib_take(s_f2))

    mean = jnp.sum(ssq[...], axis=1, keepdims=True) / WIDE
    q = qacc[...] * (lax.rsqrt(mean + 1e-06) * SCALE)
    lane_low = lax.broadcasted_iota(jnp.int32, (TOK, PAIR), 1) < HD
    for p in range(2):
        qp = q[:, p * PAIR:(p + 1) * PAIR]
        qm[2 * p] = jnp.where(lane_low, qp, 0.0).astype(BF16)
        qm[2 * p + 1] = jnp.where(lane_low, 0.0, qp).astype(BF16)

    def scores(h, j):
        at = pl.ds(pl.multiple_of(j * BLK, BLK), BLK)
        cols = slice((h // 2) * PAIR, (h // 2 + 1) * PAIR)
        s = lax.dot_general(qm[h], kc[at, cols], NT, preferred_element_type=F32)
        sbuf[h % 2, j] = s
        m = s[:, :PAIR]
        for i in range(1, BLK // PAIR):
            m = jnp.maximum(m, s[:, i * PAIR:(i + 1) * PAIR])
        mbuf[h % 2] = jnp.maximum(mbuf[h % 2], m)

    def weigh(h, j):
        at = pl.ds(pl.multiple_of(j * BLK, BLK), BLK)
        top = mbuf[2 + h % 2]
        e = [
            jnp.exp2(sbuf[h % 2, j, :, i * PAIR:(i + 1) * PAIR] - top).astype(BF16)
            for i in range(BLK // PAIR)
        ]
        e = jnp.concatenate(e, axis=1)
        obuf[h % 2] += jnp.dot(e, vp[h, at, :], preferred_element_type=F32)

    def clear(h):
        mbuf[h % 2] = jnp.full((TOK, PAIR), -3e38, F32)

    def settle(h):
        mbuf[2 + h % 2] = jnp.broadcast_to(
            jnp.max(mbuf[h % 2], axis=1, keepdims=True), (TOK, PAIR)
        )
        obuf[h % 2] = jnp.zeros((TOK, PAIR), F32)

    def stage(h_weigh, h_score):
        if h_score is not None:
            clear(h_score)

        def step(j, carry):
            if h_score is not None:
                scores(h_score, j)
            if h_weigh is not None:
                weigh(h_weigh, j)
            return carry

        lax.fori_loop(0, NB, step, 0)
        if h_score is not None:
            settle(h_score)

    def finish(p):
        top = jnp.where(lane_low, obuf[0], obuf[1])
        low = jnp.where(lane_low, obuf[1], obuf[0])
        abuf[src, p] = (top / pltpu.roll(low, HD, 1)).astype(BF16)

    def o_part(owner, p):
        w = wo[pl.ds(pl.multiple_of(owner * FEAT + p * PAIR, PAIR), PAIR), :]
        qacc[...] += jnp.dot(abuf[owner, p], w, preferred_element_type=F32)

    stage(None, 0)
    stage(0, 1)
    stage(1, None)
    finish(0)
    att.own(0)
    loads[4].wait()
    qacc[...] = jnp.zeros_like(qacc)
    o_part(src, 0)
    stage(None, 2)
    done = [(o, 0) for o in att.both(0, 1, 0)]
    stage(2, 3)
    done += [(o, 0) for o in att.both(0, 2, 0)]
    stage(3, None)
    finish(1)
    att.own(1)

    def flush():
        for o, p in done:
            o_part(o, p)
        done.clear()

    att.cross(0)
    done += [(o, 0) for o in att.both(0, 3, 0)]
    done += [(src, 1), (partner, 0)]
    flush()
    for step in (
        (0, 1, 1), (1, 1, 0), (0, 2, 1), (0, 4, 0), None, (0, 3, 1), (1, 2, 0),
        (1, 1, 1), (0, 4, 1), (1, 3, 0), (1, 2, 1), (1, 4, 0), (1, 3, 1), (1, 4, 1),
    ):
        if step is None:
            att.cross(1)
            done.append((partner, 1))
        else:
            col, dist, half = step
            done += [(o, half) for o in att.both(col, dist, half)]
        flush()

    out_ref[...] = qacc[...]
    for c in pending:
        c.wait_send()


def body(hidden_in, norm_gain, w_query, keys_cache, values_cache, lengths, w_output):
    gain = norm_gain.astype(F32).reshape(SRC, 1, FEAT)
    anywhere = pl.BlockSpec(memory_space=pl.ANY)
    vmem = pl.BlockSpec(memory_space=pltpu.VMEM)
    smem = pl.BlockSpec(memory_space=pltpu.SMEM)
    dma = pltpu.SemaphoreType.DMA
    branch = pl.pallas_call(
        kernel,
        out_shape=jax.ShapeDtypeStruct((TOK, FEAT), F32),
        in_specs=[anywhere, vmem, anywhere, anywhere, anywhere, smem, anywhere],
        out_specs=vmem,
        scratch_shapes=[
            pltpu.VMEM((SRC, TOK, FEAT), BF16),
            pltpu.VMEM((TGT, 2, POS, FEAT), BF16),
            pltpu.VMEM((WIDE, FEAT), BF16),
            pltpu.VMEM((4, WIDE, PAIR), BF16),
            pltpu.VMEM((WIDE, FEAT), BF16),
            pltpu.VMEM((WIDE, FEAT), BF16),
            pltpu.VMEM((SRC, 2, TOK, PAIR), BF16),
            pltpu.VMEM((2, NB, TOK, BLK), F32),
            pltpu.VMEM((4, TOK, PAIR), F32),
            pltpu.VMEM((2, TOK, PAIR), F32),
            pltpu.VMEM((TOK, FEAT), F32),
            pltpu.VMEM((TOK, PAIR), F32),
            pltpu.VMEM((4, TOK, PAIR), BF16),
            pltpu.VMEM((8, FEAT), F32),
            dma((5,)),
            dma((32,)), dma((32,)),
            dma((32,)), dma((32,)),
            dma((40,)), dma((32,)), dma((32,)), dma((32,)),
        ],
        compiler_params=pltpu.CompilerParams(
            collective_id=0, has_side_effects=True, vmem_limit_bytes=52 * 1024 * 1024,
        ),
        cost_estimate=pl.CostEstimate(
            flops=6_000_000_000, bytes_accessed=8_000_000, transcendentals=4_200_000
        ),
    )(hidden_in, gain, w_query, keys_cache, values_cache, lengths, w_output)
    return hidden_in.astype(F32) + branch


def solution(mesh):
    in_specs = (
        P("tgt", "src"),
        P(),
        P(None, "src"),
        P("tgt", "src"),
        P("tgt", "src"),
        P(),
        P(None, "src"),
    )
    out_specs = P("tgt", "src")
    return jax.shard_map(body, mesh=mesh, in_specs=in_specs, out_specs=out_specs, check_vma=False)
```

```python
import functools

import jax
import jax.numpy as jnp
from jax import lax
from jax.experimental import pallas as pl
from jax.experimental.pallas import tpu as pltpu
from jax.sharding import PartitionSpec as P

MESH = pl.DeviceIdType.MESH
HD = 64
NZ, NX, NYL = 8, 4, 4
SRC, TGT = 16, 32
TOK, FEAT, POS, WIDE = 256, 256, 128, 4096
PAIR = 128
HALF = 128
BLK = 512
NB = WIDE // BLK
SCALE = HD ** -0.5 * 1.4426950408889634
F32, BF16 = jnp.float32, jnp.bfloat16
NT = (((1,), (1,)), ((), ()))


def kernel(
    hid_hbm, gain_ref, wq_hbm, keys_hbm, vals_hbm, len_ref, wo_hbm, out_ref,
    hbuf, kv, kc, vp, wq, wo, abuf, sbuf, mbuf, obuf, qacc, ssq, qm, krow,
    loc_sem, h_send, h_recv, a_send, a_recv, kv_send, kv_recv,
):
    src = lax.axis_index("src")
    tgt = lax.axis_index("tgt")
    z, yh = src // 2, src % 2
    x, yl, core = tgt // 8, (tgt // 2) % 4, tgt % 2
    partner = z * 2 + (1 - yh)
    z_right = ((z + 1) % NZ) * 2 + yh
    z_left = ((z + NZ - 1) % NZ) * 2 + yh
    sib = x * 8 + yl * 2 + (1 - core)

    def at_tgt(xx, yy):
        return (xx % NX) * 8 + (yy % NYL) * 2 + core

    x_right, x_left = at_tgt(x + 1, yl), at_tgt(x + NX - 1, yl)

    loads = [
        pltpu.make_async_copy(hid_hbm, hbuf.at[src], loc_sem.at[0]),
        pltpu.make_async_copy(keys_hbm, kv.at[tgt, 0], loc_sem.at[1]),
        pltpu.make_async_copy(vals_hbm, kv.at[tgt, 1], loc_sem.at[2]),
        pltpu.make_async_copy(wq_hbm, wq, loc_sem.at[3]),
        pltpu.make_async_copy(wo_hbm, wo, loc_sem.at[4]),
    ]
    for c in loads:
        c.start()

    barrier = pltpu.get_barrier_semaphore()
    friends = [
        (partner, tgt), (z_right, tgt), (z_left, tgt),
        (src, x_right), (src, x_left), (src, sib),
        (src, at_tgt(x, yl + 1)), (src, at_tgt(x, yl + 2)), (src, at_tgt(x, yl + 3)),
    ]
    for f in friends:
        pl.semaphore_signal(barrier, inc=1, device_id=f, device_id_type=MESH)

    qacc[...] = jnp.zeros_like(qacc)
    ssq[...] = jnp.zeros_like(ssq)
    for c in loads[:3]:
        c.wait()
    pl.semaphore_wait(barrier, len(friends))

    pending = []

    def send(ref, ssem, rsem, dev):
        c = pltpu.make_async_remote_copy(
            src_ref=ref, dst_ref=ref, send_sem=ssem, recv_sem=rsem,
            device_id=dev, device_id_type=MESH,
        )
        c.start()
        pending.append(c)

    def arrived(ref, rsem):
        pltpu.make_async_remote_copy(
            src_ref=ref, dst_ref=ref, send_sem=rsem, recv_sem=rsem,
            device_id=(src, sib), device_id_type=MESH,
        ).wait_recv()

    def owner_of(col, dist, way):
        zz = (z - dist + NZ) % NZ if way == "R" else (z + dist) % NZ
        return zz * 2 + (yh if col == 0 else 1 - yh)

    class Ring:
        def __init__(self, slot, ssem, rsem):
            self.slot, self.ssem, self.rsem, self.count = slot, ssem, rsem, 0

        def push(self, owner, half, dev):
            send(self.slot(owner, half), self.ssem.at[self.count], self.rsem.at[owner * 2 + half], dev)
            self.count += 1

        def own(self, half):
            self.push(src, half, (z_right, tgt))
            self.push(src, half, (z_left, tgt))
            self.push(src, half, (partner, tgt))

        def take(self, col, dist, way, half):
            owner = owner_of(col, dist, way)
            arrived(self.slot(owner, half), self.rsem.at[owner * 2 + half])
            last = {("R", 0): 3, ("R", 1): 2, ("L", 0): 2, ("L", 1): 3}[(way, col)]
            if dist <= last:
                self.push(owner, half, (z_right if way == "R" else z_left, tgt))
            return owner

        def both(self, col, dist, half):
            ways = "RL" if dist < 4 else ("R" if col == 0 else "L")
            return [self.take(col, dist, way, half) for way in ways]

        def cross(self, half):
            arrived(self.slot(partner, half), self.rsem.at[partner * 2 + half])
            self.push(partner, half, (z_right, tgt))
            self.push(partner, half, (z_left, tgt))

    hid = Ring(lambda o, h: hbuf.at[o, pl.ds(h * HALF, HALF)], h_send, h_recv)
    att = Ring(lambda o, h: abuf.at[o, pl.ds(h * HALF, HALF)], a_send, a_recv)
    kv_count = [0]

    def kv_push(s, u, dev):
        send(kv.at[s, u], kv_send.at[kv_count[0]], kv_recv.at[s * 2 + u], dev)
        kv_count[0] += 1

    def kv_wait(s, u):
        arrived(kv.at[s, u], kv_recv.at[s * 2 + u])

    def q_part(owner):
        h = hbuf[owner].astype(F32)
        sq = h * h
        ssq[...] += sq[:, :PAIR] + sq[:, PAIR:]
        hg = (h * gain_ref[owner]).astype(BF16)
        w = wq[pl.ds(pl.multiple_of(owner * FEAT, FEAT), FEAT), :]
        qacc[...] += jnp.dot(hg, w, preferred_element_type=F32)

    def prep(s, u):
        limit = len_ref[s // 2] - (s % 2) * POS
        ok = lax.broadcasted_iota(jnp.int32, (POS, FEAT), 0) < limit
        at = pl.ds(pl.multiple_of(s * POS, POS), POS)
        data = kv[s, u].astype(F32)
        if u == 0:
            kc[at, :] = jnp.where(ok, data, krow[0:1, :]).astype(BF16)
        else:
            data = jnp.where(ok, data, 0.0).astype(BF16)
            mask = jnp.where(ok[:, :PAIR], 1.0, 0.0).astype(BF16)
            for p in range(2):
                vp[p, at, :PAIR] = data[:, p * PAIR:(p + 1) * PAIR]
                vp[p, at, PAIR:] = mask

    for half in range(2):
        hid.own(half)
    for u in range(2):
        kv_push(tgt, u, (src, x_right))
        kv_push(tgt, u, (src, x_left))
        for k in (1, 3, 2):
            kv_push(tgt, u, (src, at_tgt(x, yl + k)))
        kv_push(tgt, u, (src, sib))

    loads[3].wait()
    q_part(src)

    backlog = []

    def own_taken(s, u):
        kv_push(s, u, (src, sib))
        prep(s, u)
        backlog.append((s + 1 - 2 * core, u))

    def take_y(k, u):
        s = at_tgt(x, yl + k)
        kv_wait(s, u)
        kv_push(s, u, (src, x_right))
        kv_push(s, u, (src, x_left))
        own_taken(s, u)

    def take_x(k, u):
        s_left, s_right = at_tgt(x + NX - 1, yl + k), at_tgt(x + 1, yl + k)
        kv_wait(s_left, u)
        if u == 0:
            kv_push(s_left, u, (src, x_right))
        kv_wait(s_right, u)
        if u == 1:
            kv_push(s_right, u, (src, x_left))
        own_taken(s_left, u)
        own_taken(s_right, u)

    def take_far(k, u):
        s = at_tgt(x + 2, yl + k)
        kv_wait(s, u)
        own_taken(s, u)

    def drain(keep):
        while len(backlog) > keep:
            s, u = backlog.pop(0)
            kv_wait(s, u)
            prep(s, u)

    def first_row():
        other = tgt + 1 - 2 * core
        kv_wait(other, 0)
        even = kv[x * 8 + yl * 2, 0, 0:16, :].astype(F32)[0:1, :]
        krow[...] = jnp.broadcast_to(even, krow.shape)
        prep(tgt, 0)
        prep(tgt, 1)
        prep(other, 0)
        backlog.append((other, 1))

    def take_z(col, dist, half):
        owners = hid.both(col, dist, half)
        if half == 1:
            for o in owners:
                q_part(o)

    def cross_z():
        hid.cross(0)
        hid.cross(1)

    def cross_q():
        q_part(partner)

    Z, Y, X, W = take_z, take_y, take_x, take_far
    for event in (
        (Z, 0, 1, 0), (first_row,), (X, 0, 0), (Z, 0, 1, 1), (Y, 1, 0), (X, 0, 1),
        (Y, 3, 0), (cross_z,), (Z, 0, 2, 0), (W, 0, 0), (cross_q,), (Z, 1, 1, 0), (Y, 2, 0),
        (X, 1, 0), (Z, 0, 2, 1), (W, 0, 1), (Y, 1, 1), (Z, 1, 1, 1), (X, 3, 0),
        (W, 1, 0), (Z, 0, 3, 0), (Y, 3, 1), (X, 2, 0), (Z, 1, 2, 0), (W, 3, 0),
        (Z, 0, 3, 1), (X, 1, 1), (Y, 2, 1), (Z, 1, 2, 1), (W, 2, 0), (Z, 0, 4, 0),
        (W, 1, 1), (X, 3, 1), (Z, 1, 3, 0), (Z, 0, 4, 1), (X, 2, 1), (W, 3, 1),
        (Z, 1, 3, 1), (Z, 1, 4, 0), (W, 2, 1), (Z, 1, 4, 1),
    ):
        event[0](*event[1:])
        drain(4)
    drain(0)

    mean = jnp.sum(ssq[...], axis=1, keepdims=True) / WIDE
    q = qacc[...] * (lax.rsqrt(mean + 1e-06) * SCALE)
    low = lax.broadcasted_iota(jnp.int32, (HALF, PAIR), 1) < HD
    for t in range(2):
        for p in range(2):
            qp = q[t * HALF:(t + 1) * HALF, p * PAIR:(p + 1) * PAIR]
            qm[2 * t + p, :HALF] = jnp.where(low, qp, 0.0).astype(BF16)
            qm[2 * t + p, HALF:] = jnp.where(low, 0.0, qp).astype(BF16)

    def scores(g, j):
        p = g % 2
        keys = kc[j * BLK:(j + 1) * BLK, p * PAIR:(p + 1) * PAIR]
        s = lax.dot_general(qm[g], keys, NT, preferred_element_type=F32)
        sbuf[p, j] = s
        m = s[:, :PAIR]
        for i in range(1, BLK // PAIR):
            m = jnp.maximum(m, s[:, i * PAIR:(i + 1) * PAIR])
        mbuf[p] = m if j == 0 else jnp.maximum(mbuf[p], m)

    def weigh(g, j):
        p = g % 2
        top = mbuf[2 + p]
        e = [
            jnp.exp2(sbuf[p, j, :, i * PAIR:(i + 1) * PAIR] - top).astype(BF16)
            for i in range(BLK // PAIR)
        ]
        e = jnp.concatenate(e, axis=1)
        o = jnp.dot(e, vp[p, j * BLK:(j + 1) * BLK, :], preferred_element_type=F32)
        obuf[p] = o if j == 0 else obuf[p] + o

    def stage(g_weigh, g_score):
        for j in range(NB):
            if g_score is not None:
                scores(g_score, j)
            if g_weigh is not None:
                weigh(g_weigh, j)
        if g_score is not None:
            p = g_score % 2
            mbuf[2 + p] = jnp.broadcast_to(
                jnp.max(mbuf[p], axis=1, keepdims=True), (TOK, PAIR)
            )

    def finish(g):
        t, p = g // 2, g % 2
        o = obuf[p]
        o = o[:, :PAIR] / o[:, PAIR:]
        abuf[src, t * HALF:(t + 1) * HALF, p * PAIR:(p + 1) * PAIR] = jnp.where(
            low, o[:HALF], o[HALF:]
        ).astype(BF16)

    def o_part(owner, t):
        w = wo[pl.ds(pl.multiple_of(owner * FEAT, FEAT), FEAT), :]
        rows = slice(t * HALF, (t + 1) * HALF)
        qacc[rows, :] += jnp.dot(abuf[owner, rows, :], w, preferred_element_type=F32)

    stage(None, 0)
    stage(0, 1)
    finish(0)
    stage(1, 2)
    finish(1)
    att.own(0)
    stage(2, 3)
    finish(2)
    stage(3, None)
    finish(3)
    att.own(1)
    loads[4].wait()
    qacc[...] = jnp.zeros_like(qacc)
    o_part(src, 0)
    o_part(src, 1)
    for step in (
        (0, 1, 0), (0, 1, 1), 0, (0, 2, 0), 1, (0, 2, 1), (1, 1, 0), (0, 3, 0), (1, 1, 1),
        (0, 3, 1), (1, 2, 0), (0, 4, 0), (1, 2, 1), (0, 4, 1), (1, 3, 0), (1, 3, 1),
        (1, 4, 0), (1, 4, 1),
    ):
        if isinstance(step, int):
            att.cross(step)
            o_part(partner, step)
        else:
            for o in att.both(*step):
                o_part(o, step[2])

    out_ref[...] = qacc[...]
    for c in pending:
        c.wait_send()


def body(hidden_in, norm_gain, w_query, keys_cache, values_cache, lengths, w_output):
    gain = norm_gain.astype(F32).reshape(SRC, 1, FEAT)
    anywhere = pl.BlockSpec(memory_space=pl.ANY)
    vmem = pl.BlockSpec(memory_space=pltpu.VMEM)
    smem = pl.BlockSpec(memory_space=pltpu.SMEM)
    dma = pltpu.SemaphoreType.DMA
    branch = pl.pallas_call(
        kernel,
        out_shape=jax.ShapeDtypeStruct((TOK, FEAT), F32),
        in_specs=[anywhere, vmem, anywhere, anywhere, anywhere, smem, anywhere],
        out_specs=vmem,
        scratch_shapes=[
            pltpu.VMEM((SRC, TOK, FEAT), BF16),
            pltpu.VMEM((TGT, 2, POS, FEAT), BF16),
            pltpu.VMEM((WIDE, FEAT), BF16),
            pltpu.VMEM((2, WIDE, FEAT), BF16),
            pltpu.VMEM((WIDE, FEAT), BF16),
            pltpu.VMEM((WIDE, FEAT), BF16),
            pltpu.VMEM((SRC, TOK, FEAT), BF16),
            pltpu.VMEM((2, NB, TOK, BLK), F32),
            pltpu.VMEM((4, TOK, PAIR), F32),
            pltpu.VMEM((2, TOK, FEAT), F32),
            pltpu.VMEM((TOK, FEAT), F32),
            pltpu.VMEM((TOK, PAIR), F32),
            pltpu.VMEM((4, TOK, PAIR), BF16),
            pltpu.VMEM((8, FEAT), F32),
            dma((5,)),
            dma((32,)), dma((32,)),
            dma((32,)), dma((32,)),
            dma((80,)), dma((64,)),
        ],
        compiler_params=pltpu.CompilerParams(
            collective_id=0, has_side_effects=True, vmem_limit_bytes=63 * 1024 * 1024,
        ),
        cost_estimate=pl.CostEstimate(
            flops=6_000_000_000, bytes_accessed=8_000_000, transcendentals=4_200_000
        ),
    )(hidden_in, gain, w_query, keys_cache, values_cache, lengths, w_output)
    return hidden_in.astype(F32) + branch


def solution(mesh):
    in_specs = (
        P("tgt", "src"),
        P(),
        P(None, "src"),
        P("tgt", "src"),
        P("tgt", "src"),
        P(),
        P(None, "src"),
    )
    out_specs = P("tgt", "src")
    return jax.shard_map(body, mesh=mesh, in_specs=in_specs, out_specs=out_specs, check_vma=False)
```

```python
import functools

import jax
import jax.numpy as jnp
from jax import lax
from jax.experimental import pallas as pl
from jax.experimental.pallas import tpu as pltpu
from jax.sharding import PartitionSpec as P

MESH = pl.DeviceIdType.MESH
HD = 64
NZ, NX, NYL = 8, 4, 4
SRC, TGT = 16, 32
TOK, FEAT, POS, WIDE = 256, 256, 128, 4096
PAIR = 128
HALF = 128
LAG = 6
BLK = 512
NB = WIDE // BLK
SCALE = HD ** -0.5 * 1.4426950408889634
F32, BF16 = jnp.float32, jnp.bfloat16
NT = (((1,), (1,)), ((), ()))


def kernel(
    hid_hbm, gain_ref, wq_hbm, keys_hbm, vals_hbm, len_ref, wo_hbm, out_ref,
    hbuf, kv, kc, vp, wq, wo, wop, abuf, sbuf, mbuf, obuf, qacc, pacc, pbuf, rbuf, ssq, qm, krow,
    loc_sem, h_send, h_recv, a_send, a_recv, kv_send, kv_recv, w_send, w_recv, p_send, p_recv,
):
    src = lax.axis_index("src")
    tgt = lax.axis_index("tgt")
    z, yh = src // 2, src % 2
    x, yl, core = tgt // 8, (tgt // 2) % 4, tgt % 2
    partner = z * 2 + (1 - yh)
    z_right = ((z + 1) % NZ) * 2 + yh
    z_left = ((z + NZ - 1) % NZ) * 2 + yh
    sib = x * 8 + yl * 2 + (1 - core)

    def at_tgt(xx, yy):
        return (xx % NX) * 8 + (yy % NYL) * 2 + core

    x_right, x_left = at_tgt(x + 1, yl), at_tgt(x + NX - 1, yl)

    loads = [
        pltpu.make_async_copy(hid_hbm, hbuf.at[src], loc_sem.at[0]),
        pltpu.make_async_copy(keys_hbm, kv.at[tgt, 0], loc_sem.at[1]),
        pltpu.make_async_copy(vals_hbm, kv.at[tgt, 1], loc_sem.at[2]),
        pltpu.make_async_copy(wq_hbm, wq, loc_sem.at[3]),
        pltpu.make_async_copy(wo_hbm, wo, loc_sem.at[4]),
    ]
    for c in loads:
        c.start()

    barrier = pltpu.get_barrier_semaphore()
    friends = [
        (partner, tgt), (z_right, tgt), (z_left, tgt),
        (src, x_right), (src, x_left), (src, sib),
        (src, at_tgt(x, yl + 1)), (src, at_tgt(x, yl + 2)), (src, at_tgt(x, yl + 3)),
    ]
    for f in friends:
        pl.semaphore_signal(barrier, inc=1, device_id=f, device_id_type=MESH)

    qacc[...] = jnp.zeros_like(qacc)
    ssq[...] = jnp.zeros_like(ssq)
    for c in loads[:3]:
        c.wait()
    pl.semaphore_wait(barrier, len(friends))

    pending = []

    def send(ref, ssem, rsem, dev):
        c = pltpu.make_async_remote_copy(
            src_ref=ref, dst_ref=ref, send_sem=ssem, recv_sem=rsem,
            device_id=dev, device_id_type=MESH,
        )
        c.start()
        pending.append(c)

    def arrived(ref, rsem):
        pltpu.make_async_remote_copy(
            src_ref=ref, dst_ref=ref, send_sem=rsem, recv_sem=rsem,
            device_id=(src, sib), device_id_type=MESH,
        ).wait_recv()

    def owner_of(col, dist, way):
        zz = (z - dist + NZ) % NZ if way == "R" else (z + dist) % NZ
        return zz * 2 + (yh if col == 0 else 1 - yh)

    class Ring:
        def __init__(self, slot, ssem, rsem):
            self.slot, self.ssem, self.rsem, self.count = slot, ssem, rsem, 0

        def push(self, owner, half, dev):
            send(self.slot(owner, half), self.ssem.at[self.count], self.rsem.at[owner * 2 + half], dev)
            self.count += 1

        def own(self, half):
            self.push(src, half, (z_right, tgt))
            self.push(src, half, (z_left, tgt))
            self.push(src, half, (partner, tgt))

        def take(self, col, dist, way, half):
            owner = owner_of(col, dist, way)
            arrived(self.slot(owner, half), self.rsem.at[owner * 2 + half])
            last = {("R", 0): 3, ("R", 1): 2, ("L", 0): 2, ("L", 1): 3}[(way, col)]
            if dist <= last:
                self.push(owner, half, (z_right if way == "R" else z_left, tgt))
            return owner

        def cross(self, half):
            arrived(self.slot(partner, half), self.rsem.at[partner * 2 + half])
            self.push(partner, half, (z_right, tgt))
            self.push(partner, half, (z_left, tgt))

    hid = Ring(lambda o, h: hbuf.at[o, pl.ds(h * HALF, HALF)], h_send, h_recv)
    kv_count, a_count, w_count = [0], [0], [0]

    def kv_push(s, u, dev):
        send(kv.at[s, u], kv_send.at[kv_count[0]], kv_recv.at[s * 2 + u], dev)
        kv_count[0] += 1

    def kv_wait(s, u):
        arrived(kv.at[s, u], kv_recv.at[s * 2 + u])

    def q_part(owner):
        h = hbuf[owner].astype(F32)
        sq = h * h
        ssq[...] += sq[:, :PAIR] + sq[:, PAIR:]
        hg = (h * gain_ref[owner]).astype(BF16)
        w = wq[pl.ds(pl.multiple_of(owner * FEAT, FEAT), FEAT), :]
        qacc[...] += jnp.dot(hg, w, preferred_element_type=F32)

    def prep(s, u):
        limit = len_ref[s // 2] - (s % 2) * POS
        ok = lax.broadcasted_iota(jnp.int32, (POS, FEAT), 0) < limit
        at = pl.ds(pl.multiple_of(s * POS, POS), POS)
        data = kv[s, u].astype(F32)
        if u == 0:
            kc[at, :] = jnp.where(ok, data, krow[0:1, :]).astype(BF16)
        else:
            data = jnp.where(ok, data, 0.0).astype(BF16)
            mask = jnp.where(ok[:, :PAIR], 1.0, 0.0).astype(BF16)
            for p in range(2):
                vp[p, at, :PAIR] = data[:, p * PAIR:(p + 1) * PAIR]
                vp[p, at, PAIR:] = mask

    for half in range(2):
        hid.own(half)
    def own_y(u):
        for k in (1, 3, 2):
            kv_push(tgt, u, (src, at_tgt(x, yl + k)))

    for u in range(2):
        kv_push(tgt, u, (src, x_right))
        kv_push(tgt, u, (src, x_left))
        kv_push(tgt, u, (src, sib))
    own_y(0)

    loads[3].wait()
    q_part(src)

    backlog = []

    def own_taken(s, u):
        kv_push(s, u, (src, sib))
        prep(s, u)
        backlog.append((s + 1 - 2 * core, u))

    def take_y(k, u):
        s = at_tgt(x, yl + k)
        kv_wait(s, u)
        kv_push(s, u, (src, x_right))
        kv_push(s, u, (src, x_left))
        own_taken(s, u)

    def take_x(k, u, way):
        from_left = way == "l"
        s = at_tgt(x + NX - 1 if from_left else x + 1, yl + k)
        kv_wait(s, u)
        far_right = (k in (0, 3)) == (u == 0)
        if from_left and far_right:
            kv_push(s, u, (src, x_right))
        if not from_left and not far_right:
            kv_push(s, u, (src, x_left))
        own_taken(s, u)

    def take_far(k, u):
        s = at_tgt(x + 2, yl + k)
        kv_wait(s, u)
        own_taken(s, u)

    def drain(keep):
        while len(backlog) > keep:
            s, u = backlog.pop(0)
            kv_wait(s, u)
            prep(s, u)

    def first_row():
        other = tgt + 1 - 2 * core
        kv_wait(other, 0)
        even = kv[x * 8 + yl * 2, 0, 0:16, :].astype(F32)[0:1, :]
        krow[...] = jnp.broadcast_to(even, krow.shape)
        prep(tgt, 0)
        prep(tgt, 1)
        prep(other, 0)
        backlog.append((other, 1))

    halves = {}

    def counted(key, owner):
        halves[key] = halves.get(key, 0) + 1
        if halves[key] == 2:
            q_part(owner)

    def take_z(col, dist, half, way):
        counted((col, dist, way), hid.take(col, dist, way, half))

    def cross_z(half):
        hid.cross(half)
        counted("cross", partner)

    def wo_block(xx):
        return (xx % NX) * 2 + core

    def w_push(j, h, dev, ref=None):
        dst = wop.at[j, pl.ds(h * HALF, HALF)]
        c = pltpu.make_async_remote_copy(
            src_ref=dst if ref is None else ref, dst_ref=dst,
            send_sem=w_send.at[w_count[0]], recv_sem=w_recv.at[j * 2 + h],
            device_id=dev, device_id_type=MESH,
        )
        c.start()
        pending.append(c)
        w_count[0] += 1

    def w_wait(j, h):
        arrived(wop.at[j, pl.ds(h * HALF, HALF)], w_recv.at[j * 2 + h])

    def send_wo():
        j = wo_block(x)
        loads[4].wait()
        for h in range(2):
            row = pl.multiple_of((j * 2 + 1 - yh) * FEAT + h * HALF, HALF)
            w_push(j, h, (partner, tgt), wo.at[pl.ds(row, HALF)])

    def share_wo():
        j = wo_block(x)
        for h in range(2):
            w_wait(j, h)
            w_push(j, h, (src, x_right))
            w_push(j, h, (src, x_left))
            w_push(j, h, (src, sib))

    def share_wo_x():
        j_left, j_right = wo_block(x + NX - 1), wo_block(x + 1)
        w_wait(j_left, 0)
        w_push(j_left, 0, (src, x_right))
        w_wait(j_right, 1)
        w_push(j_right, 1, (src, x_left))
        w_wait(j_left, 1)
        w_wait(j_right, 0)
        for h in range(2):
            w_push(j_left, h, (src, sib))
            w_push(j_right, h, (src, sib))

    def share_wo_far():
        j = wo_block(x + 2)
        for h in range(2):
            w_wait(j, h)
            w_push(j, h, (src, sib))

    def share_wo_end():
        for xx in range(NX):
            for h in range(2):
                w_wait(xx * 2 + 1 - core, h)

    Z, C, F, Y, X, W, O = take_z, cross_z, first_row, take_y, take_x, take_far, send_wo
    V = functools.partial(own_y, 1)
    for event in (
        (Z, 0, 1, 0, "R"), (F,), (X, 0, 0, "r"), (Z, 0, 1, 0, "L"), (V,), (X, 0, 0, "l"), (Z, 0, 1, 1, "R"),
        (X, 0, 1, "l"), (Z, 0, 1, 1, "L"), (Z, 0, 2, 0, "R"), (X, 0, 1, "r"), (Z, 0, 2, 0, "L"),
        (Z, 0, 2, 1, "R"), (W, 0, 0), (Z, 0, 2, 1, "L"), (Y, 3, 0), (C, 0), (Y, 1, 0), (W, 0, 1), (Y, 2, 0),
        (C, 1), (Z, 0, 3, 0, "R"), (Z, 0, 3, 1, "R"), (Z, 0, 3, 1, "L"), (X, 3, 0, "l"), (X, 3, 0, "r"),
        (Z, 1, 1, 0, "L"), (Z, 0, 3, 0, "L"), (X, 1, 0, "r"), (Z, 1, 1, 1, "R"), (Z, 1, 1, 0, "R"),
        (Z, 1, 1, 1, "L"), (Y, 1, 1), (Y, 3, 1), (Y, 2, 1), (Z, 1, 2, 0, "L"), (W, 3, 0), (O,), (X, 2, 0, "l"),
        (Z, 0, 4, 1, "R"), (X, 2, 0, "r"), (Z, 1, 2, 1, "L"), (W, 1, 0), (X, 1, 0, "l"), (Z, 1, 2, 1, "R"),
        (X, 1, 1, "l"), (Z, 0, 4, 0, "R"), (X, 1, 1, "r"), (Z, 1, 3, 0, "L"), (X, 3, 1, "r"), (Z, 1, 2, 0, "R"),
        (X, 2, 1, "l"), (Z, 1, 3, 1, "L"), (X, 3, 1, "l"), (Z, 1, 3, 1, "R"), (W, 1, 1), (W, 2, 0),
        (X, 2, 1, "r"), (Z, 1, 4, 0, "L"), (Z, 1, 3, 0, "R"), (W, 2, 1), (W, 3, 1), (Z, 1, 4, 1, "L"),
    ):
        event[0](*event[1:])
        drain(LAG)
    drain(0)

    mean = jnp.sum(ssq[...], axis=1, keepdims=True) / WIDE
    q = qacc[...] * (lax.rsqrt(mean + 1e-06) * SCALE)
    low = lax.broadcasted_iota(jnp.int32, (HALF, PAIR), 1) < HD
    for t in range(2):
        for p in range(2):
            qp = q[t * HALF:(t + 1) * HALF, p * PAIR:(p + 1) * PAIR]
            qm[2 * t + p, :HALF] = jnp.where(low, qp, 0.0).astype(BF16)
            qm[2 * t + p, HALF:] = jnp.where(low, 0.0, qp).astype(BF16)

    def scores(g, j):
        p = g % 2
        keys = kc[j * BLK:(j + 1) * BLK, p * PAIR:(p + 1) * PAIR]
        s = lax.dot_general(qm[g], keys, NT, preferred_element_type=F32)
        sbuf[p, j] = s
        m = s[:, :PAIR]
        for i in range(1, BLK // PAIR):
            m = jnp.maximum(m, s[:, i * PAIR:(i + 1) * PAIR])
        mbuf[p] = m if j == 0 else jnp.maximum(mbuf[p], m)

    def weigh(g, j):
        p = g % 2
        top = mbuf[2 + p]
        e = [
            jnp.exp2(sbuf[p, j, :, i * PAIR:(i + 1) * PAIR] - top).astype(BF16)
            for i in range(BLK // PAIR)
        ]
        e = jnp.concatenate(e, axis=1)
        o = jnp.dot(e, vp[p, j * BLK:(j + 1) * BLK, :], preferred_element_type=F32)
        obuf[p] = o if j == 0 else obuf[p] + o

    def stage(g_weigh, g_score):
        for j in range(NB):
            if g_score is not None:
                scores(g_score, j)
            if g_weigh is not None:
                weigh(g_weigh, j)
        if g_score is not None:
            p = g_score % 2
            mbuf[2 + p] = jnp.broadcast_to(
                jnp.max(mbuf[p], axis=1, keepdims=True), (TOK, PAIR)
            )

    def finish(g):
        t, p = g // 2, g % 2
        o = obuf[p]
        o = o[:, :PAIR] / o[:, PAIR:]
        abuf[z, t * HALF:(t + 1) * HALF, p * PAIR:(p + 1) * PAIR] = jnp.where(
            low, o[:HALF], o[HALF:]
        ).astype(BF16)

    def a_push(zz, t, dev):
        ref = abuf.at[zz, pl.ds(t * HALF, HALF)]
        send(ref, a_send.at[a_count[0]], a_recv.at[zz * 2 + t], dev)
        a_count[0] += 1

    def a_own(t):
        a_push(z, t, (z_right, tgt))
        a_push(z, t, (z_left, tgt))

    def o_part(zz, t):
        rows = slice(t * HALF, (t + 1) * HALF)
        a = abuf[zz, rows, :]
        w = wo[pl.ds(pl.multiple_of((zz * 2 + yh) * FEAT, FEAT), FEAT), :]
        qacc[rows, :] += jnp.dot(a, w, preferred_element_type=F32)
        pacc[rows, :] += jnp.dot(a, wop[zz], preferred_element_type=F32)

    def a_take(dist, t):
        taken = []
        for way in "RL" if dist < 4 else "RL"[t]:
            zz = (z - dist + NZ) % NZ if way == "R" else (z + dist) % NZ
            arrived(abuf.at[zz, pl.ds(t * HALF, HALF)], a_recv.at[zz * 2 + t])
            if dist < 3 or (dist == 3 and way == "RL"[t]):
                a_push(zz, t, (z_right if way == "R" else z_left, tgt))
            taken.append(zz)
        for zz in taken:
            o_part(zz, t)

    def exchange(t):
        pbuf[t] = pacc[t * HALF:(t + 1) * HALF, :].astype(BF16)
        c = pltpu.make_async_remote_copy(
            src_ref=pbuf.at[t], dst_ref=rbuf.at[t], send_sem=p_send.at[t], recv_sem=p_recv.at[t],
            device_id=(partner, tgt), device_id_type=MESH,
        )
        c.start()
        pending.append(c)

    stage(None, 0)
    share_wo()
    stage(0, 1)
    finish(0)
    stage(1, 2)
    finish(1)
    a_own(0)
    share_wo_x()
    stage(2, 3)
    finish(2)
    stage(3, None)
    finish(3)
    a_own(1)
    share_wo_far()
    qacc[...] = jnp.zeros_like(qacc)
    pacc[...] = jnp.zeros_like(pacc)
    share_wo_end()
    o_part(z, 0)
    o_part(z, 1)
    for dist, t in ((1, 0), (1, 1), (2, 0), (2, 1), (3, 0), (3, 1), (4, 0)):
        a_take(dist, t)
    exchange(0)
    a_take(4, 1)
    exchange(1)
    for t in range(2):
        arrived(rbuf.at[t], p_recv.at[t])
        rows = slice(t * HALF, (t + 1) * HALF)
        out_ref[rows, :] = qacc[rows, :] + rbuf[t].astype(F32)
    for c in pending:
        c.wait_send()


def body(hidden_in, norm_gain, w_query, keys_cache, values_cache, lengths, w_output):
    gain = norm_gain.astype(F32).reshape(SRC, 1, FEAT)
    anywhere = pl.BlockSpec(memory_space=pl.ANY)
    vmem = pl.BlockSpec(memory_space=pltpu.VMEM)
    smem = pl.BlockSpec(memory_space=pltpu.SMEM)
    dma = pltpu.SemaphoreType.DMA
    branch = pl.pallas_call(
        kernel,
        out_shape=jax.ShapeDtypeStruct((TOK, FEAT), F32),
        in_specs=[anywhere, vmem, anywhere, anywhere, anywhere, smem, anywhere],
        out_specs=vmem,
        scratch_shapes=[
            pltpu.VMEM((SRC, TOK, FEAT), BF16),
            pltpu.VMEM((TGT, 2, POS, FEAT), BF16),
            pltpu.VMEM((WIDE, FEAT), BF16),
            pltpu.VMEM((2, WIDE, FEAT), BF16),
            pltpu.VMEM((WIDE, FEAT), BF16),
            pltpu.VMEM((WIDE, FEAT), BF16),
            pltpu.VMEM((NZ, FEAT, FEAT), BF16),
            pltpu.VMEM((NZ, TOK, FEAT), BF16),
            pltpu.VMEM((2, NB, TOK, BLK), F32),
            pltpu.VMEM((4, TOK, PAIR), F32),
            pltpu.VMEM((2, TOK, FEAT), F32),
            pltpu.VMEM((TOK, FEAT), F32),
            pltpu.VMEM((TOK, FEAT), F32),
            pltpu.VMEM((2, HALF, FEAT), BF16),
            pltpu.VMEM((2, HALF, FEAT), BF16),
            pltpu.VMEM((TOK, PAIR), F32),
            pltpu.VMEM((4, TOK, PAIR), BF16),
            pltpu.VMEM((8, FEAT), F32),
            dma((5,)),
            dma((32,)), dma((32,)),
            dma((16,)), dma((16,)),
            dma((80,)), dma((64,)), dma((20,)), dma((16,)), dma((2,)), dma((2,)),
        ],
        compiler_params=pltpu.CompilerParams(
            collective_id=0, has_side_effects=True, vmem_limit_bytes=63 * 1024 * 1024,
        ),
        cost_estimate=pl.CostEstimate(
            flops=6_000_000_000, bytes_accessed=8_000_000, transcendentals=4_200_000
        ),
    )(hidden_in, gain, w_query, keys_cache, values_cache, lengths, w_output)
    return hidden_in.astype(F32) + branch


def solution(mesh):
    in_specs = (
        P("tgt", "src"),
        P(),
        P(None, "src"),
        P("tgt", "src"),
        P("tgt", "src"),
        P(),
        P(None, "src"),
    )
    out_specs = P("tgt", "src")
    return jax.shard_map(body, mesh=mesh, in_specs=in_specs, out_specs=out_specs, check_vma=False)
```

```python
import functools

import jax
import jax.numpy as jnp
from jax import lax
from jax.experimental import pallas as pl
from jax.experimental.pallas import tpu as pltpu
from jax.sharding import PartitionSpec as P

MESH = pl.DeviceIdType.MESH
HD = 64
NZ, NX, NYL = 8, 4, 4
SRC, TGT = 16, 32
TOK, FEAT, POS, WIDE = 256, 256, 128, 4096
PAIR = 128
HALF = 128
LAG = 6
BLK = 512
NB = WIDE // BLK
SCALE = HD ** -0.5 * 1.4426950408889634
F32, BF16 = jnp.float32, jnp.bfloat16
NT = (((1,), (1,)), ((), ()))


def kernel(
    hid_hbm, gain_ref, wq_hbm, keys_hbm, vals_hbm, len_ref, wo_hbm, out_ref,
    hbuf, kv, kc, vp, wq, wo, wop, abuf, sbuf, mbuf, obuf, qacc, pacc, pbuf, rbuf, ssq, qm, krow,
    loc_sem, h_send, h_recv, a_send, a_recv, kv_send, kv_recv, w_send, w_recv, p_send, p_recv,
):
    src = lax.axis_index("src")
    tgt = lax.axis_index("tgt")
    z, yh = src // 2, src % 2
    x, yl, core = tgt // 8, (tgt // 2) % 4, tgt % 2
    partner = z * 2 + (1 - yh)
    z_right = ((z + 1) % NZ) * 2 + yh
    z_left = ((z + NZ - 1) % NZ) * 2 + yh
    sib = x * 8 + yl * 2 + (1 - core)

    def at_tgt(xx, yy):
        return (xx % NX) * 8 + (yy % NYL) * 2 + core

    x_right, x_left = at_tgt(x + 1, yl), at_tgt(x + NX - 1, yl)
    edge = yl == 0
    rows_from = [
        yl,
        jnp.where(edge, 1, yl - 1),
        jnp.where(edge, 2, jnp.where(yl == 3, 1, yl + 1)),
        jnp.where(yl < 2, 3, 0),
    ]

    loads = [
        pltpu.make_async_copy(hid_hbm, hbuf.at[src], loc_sem.at[0]),
        pltpu.make_async_copy(keys_hbm, kv.at[tgt, 0], loc_sem.at[1]),
        pltpu.make_async_copy(vals_hbm, kv.at[tgt, 1], loc_sem.at[2]),
        pltpu.make_async_copy(wq_hbm, wq, loc_sem.at[3]),
        pltpu.make_async_copy(wo_hbm, wo, loc_sem.at[4]),
    ]
    for c in loads:
        c.start()

    barrier = pltpu.get_barrier_semaphore()
    friends = [
        (partner, tgt), (z_right, tgt), (z_left, tgt),
        (src, x_right), (src, x_left), (src, sib),
        (src, at_tgt(x, yl + 1)), (src, at_tgt(x, yl + NYL - 1)),
    ]
    for f in friends:
        pl.semaphore_signal(barrier, inc=1, device_id=f, device_id_type=MESH)

    qacc[...] = jnp.zeros_like(qacc)
    ssq[...] = jnp.zeros_like(ssq)
    for c in loads[:3]:
        c.wait()
    pl.semaphore_wait(barrier, len(friends))

    pending, guarded = [], []

    def send(ref, ssem, rsem, dev):
        c = pltpu.make_async_remote_copy(
            src_ref=ref, dst_ref=ref, send_sem=ssem, recv_sem=rsem,
            device_id=dev, device_id_type=MESH,
        )
        c.start()
        pending.append(c)

    def arrived(ref, rsem):
        pltpu.make_async_remote_copy(
            src_ref=ref, dst_ref=ref, send_sem=rsem, recv_sem=rsem,
            device_id=(src, sib), device_id_type=MESH,
        ).wait_recv()

    def owner_of(col, dist, way):
        zz = (z - dist + NZ) % NZ if way == "R" else (z + dist) % NZ
        return zz * 2 + (yh if col == 0 else 1 - yh)

    class Ring:
        def __init__(self, slot, ssem, rsem):
            self.slot, self.ssem, self.rsem, self.count = slot, ssem, rsem, 0

        def push(self, owner, half, dev):
            send(self.slot(owner, half), self.ssem.at[self.count], self.rsem.at[owner * 2 + half], dev)
            self.count += 1

        def own(self, half):
            self.push(src, half, (z_right, tgt))
            self.push(src, half, (z_left, tgt))
            self.push(src, half, (partner, tgt))

        def take(self, col, dist, way, half):
            owner = owner_of(col, dist, way)
            arrived(self.slot(owner, half), self.rsem.at[owner * 2 + half])
            last = {("R", 0): 3, ("R", 1): 2, ("L", 0): 2, ("L", 1): 3}[(way, col)]
            if dist <= last:
                self.push(owner, half, (z_right if way == "R" else z_left, tgt))
            return owner

        def cross(self, half):
            arrived(self.slot(partner, half), self.rsem.at[partner * 2 + half])
            self.push(partner, half, (z_right, tgt))
            self.push(partner, half, (z_left, tgt))

    hid = Ring(lambda o, h: hbuf.at[o, pl.ds(h * HALF, HALF)], h_send, h_recv)
    kv_count, a_count, w_count = [0], [0], [0]

    def kv_push(s, u, dev):
        send(kv.at[s, u], kv_send.at[kv_count[0]], kv_recv.at[s * 2 + u], dev)
        kv_count[0] += 1

    def kv_wait(s, u):
        arrived(kv.at[s, u], kv_recv.at[s * 2 + u])

    def q_part(owner):
        h = hbuf[owner].astype(F32)
        sq = h * h
        ssq[...] += sq[:, :PAIR] + sq[:, PAIR:]
        hg = (h * gain_ref[owner]).astype(BF16)
        w = wq[pl.ds(pl.multiple_of(owner * FEAT, FEAT), FEAT), :]
        qacc[...] += jnp.dot(hg, w, preferred_element_type=F32)

    def prep(s, u):
        limit = len_ref[s // 2] - (s % 2) * POS
        ok = lax.broadcasted_iota(jnp.int32, (POS, FEAT), 0) < limit
        at = pl.ds(pl.multiple_of(s * POS, POS), POS)
        data = kv[s, u].astype(F32)
        if u == 0:
            kc[at, :] = jnp.where(ok, data, krow[0:1, :]).astype(BF16)
        else:
            data = jnp.where(ok, data, 0.0).astype(BF16)
            mask = jnp.where(ok[:, :PAIR], 1.0, 0.0).astype(BF16)
            for p in range(2):
                vp[p, at, :PAIR] = data[:, p * PAIR:(p + 1) * PAIR]
                vp[p, at, PAIR:] = mask

    for half in range(2):
        hid.own(half)
    def at_yl(yy):
        return x * 8 + yy * 2 + core

    def maybe(when, s, u, dev):
        i = kv_count[0]
        kv_count[0] += 1
        c = pltpu.make_async_remote_copy(
            src_ref=kv.at[s, u], dst_ref=kv.at[s, u], send_sem=kv_send.at[i],
            recv_sem=kv_recv.at[s * 2 + u], device_id=dev, device_id_type=MESH,
        )
        pl.when(when)(c.start)
        guarded.append((when, c))

    for u in range(2):
        maybe(yl < NYL - 1, tgt, u, (src, at_yl(jnp.minimum(yl + 1, NYL - 1))))
        maybe(yl > 0, tgt, u, (src, at_yl(jnp.maximum(yl - 1, 0))))
        kv_push(tgt, u, (src, x_right))
        kv_push(tgt, u, (src, x_left))
        kv_push(tgt, u, (src, sib))
    inner = (yl > 0) & (yl < NYL - 1)

    loads[3].wait()
    q_part(src)

    backlog = []

    def own_taken(s, u):
        kv_push(s, u, (src, sib))
        prep(s, u)
        backlog.append((s + 1 - 2 * core, u))

    def take_y(k, u):
        s = at_yl(rows_from[k])
        kv_wait(s, u)
        onward = jnp.where(rows_from[k] > yl, yl - 1, yl + 1)
        maybe(inner, s, u, (src, at_yl(jnp.clip(onward, 0, NYL - 1))))
        kv_push(s, u, (src, x_right))
        kv_push(s, u, (src, x_left))
        own_taken(s, u)

    def take_x(k, u, way):
        from_left = way == "l"
        s = at_tgt(x + NX - 1 if from_left else x + 1, rows_from[k])
        kv_wait(s, u)
        far_right = (k in (0, 3)) == (u == 0)
        if from_left and far_right:
            kv_push(s, u, (src, x_right))
        if not from_left and not far_right:
            kv_push(s, u, (src, x_left))
        own_taken(s, u)

    def take_far(k, u):
        s = at_tgt(x + 2, rows_from[k])
        kv_wait(s, u)
        own_taken(s, u)

    def drain(keep, only=None):
        spare = len(backlog) - keep if only is None else len(backlog)
        kept = []
        for i, (s, u) in enumerate(backlog):
            if i < spare and only in (None, u):
                kv_wait(s, u)
                prep(s, u)
            else:
                kept.append((s, u))
        backlog[:] = kept

    def first_row():
        other = tgt + 1 - 2 * core
        kv_wait(other, 0)
        even = kv[x * 8 + yl * 2, 0, 0:16, :].astype(F32)[0:1, :]
        krow[...] = jnp.broadcast_to(even, krow.shape)
        prep(tgt, 0)
        prep(tgt, 1)
        prep(other, 0)
        backlog.append((other, 1))

    halves = {}

    def counted(key, owner):
        halves[key] = halves.get(key, 0) + 1
        if halves[key] == 2:
            q_part(owner)

    def take_z(col, dist, half, way):
        counted((col, dist, way), hid.take(col, dist, way, half))

    def cross_z(half):
        hid.cross(half)
        counted("cross", partner)

    def wo_block(xx):
        return (xx % NX) * 2 + core

    def w_push(j, h, dev, ref=None):
        dst = wop.at[j, pl.ds(h * HALF, HALF)]
        c = pltpu.make_async_remote_copy(
            src_ref=dst if ref is None else ref, dst_ref=dst,
            send_sem=w_send.at[w_count[0]], recv_sem=w_recv.at[j * 2 + h],
            device_id=dev, device_id_type=MESH,
        )
        c.start()
        pending.append(c)
        w_count[0] += 1

    def w_wait(j, h):
        arrived(wop.at[j, pl.ds(h * HALF, HALF)], w_recv.at[j * 2 + h])

    def send_wo():
        j = wo_block(x)
        loads[4].wait()
        for h in range(2):
            row = pl.multiple_of((j * 2 + 1 - yh) * FEAT + h * HALF, HALF)
            w_push(j, h, (partner, tgt), wo.at[pl.ds(row, HALF)])

    def take_wo(h):
        j = wo_block(x)
        w_wait(j, h)
        w_push(j, h, (src, x_right))
        w_push(j, h, (src, x_left))
        w_push(j, h, (src, sib))

    def take_wo_x(h, way):
        j = wo_block(x + NX - 1 if way == "l" else x + 1)
        w_wait(j, h)
        if (h, way) == (0, "l"):
            w_push(j, h, (src, x_right))
        if (h, way) == (1, "r"):
            w_push(j, h, (src, x_left))
        w_push(j, h, (src, sib))

    def take_wo_far(h):
        j = wo_block(x + 2)
        w_wait(j, h)
        w_push(j, h, (src, sib))

    ready, todo = [], []

    def flush():
        while ready and todo:
            o_part(*todo.pop(0))

    def end_wo():
        for xx in range(NX):
            for h in range(2):
                w_wait(xx * 2 + 1 - core, h)
        ready.append(1)
        flush()

    low = lax.broadcasted_iota(jnp.int32, (HALF, PAIR), 1) < HD

    def make_queries():
        mean = jnp.sum(ssq[...], axis=1, keepdims=True) / WIDE
        q = qacc[...] * (lax.rsqrt(mean + 1e-06) * SCALE)
        for t in range(2):
            for p in range(2):
                qp = q[t * HALF:(t + 1) * HALF, p * PAIR:(p + 1) * PAIR]
                qm[2 * t + p, :HALF] = jnp.where(low, qp, 0.0).astype(BF16)
                qm[2 * t + p, HALF:] = jnp.where(low, 0.0, qp).astype(BF16)
        qacc[...] = jnp.zeros_like(qacc)
        pacc[...] = jnp.zeros_like(pacc)

    def scores(g, j):
        p = g % 2
        keys = kc[j * BLK:(j + 1) * BLK, p * PAIR:(p + 1) * PAIR]
        s = lax.dot_general(qm[g], keys, NT, preferred_element_type=F32)
        sbuf[p, j] = s
        m = s[:, :PAIR]
        for i in range(1, BLK // PAIR):
            m = jnp.maximum(m, s[:, i * PAIR:(i + 1) * PAIR])
        mbuf[p] = m if j == 0 else jnp.maximum(mbuf[p], m)

    def weigh(g, j):
        p = g % 2
        top = mbuf[2 + p]
        e = [
            jnp.exp2(sbuf[p, j, :, i * PAIR:(i + 1) * PAIR] - top).astype(BF16)
            for i in range(BLK // PAIR)
        ]
        e = jnp.concatenate(e, axis=1)
        o = jnp.dot(e, vp[p, j * BLK:(j + 1) * BLK, :], preferred_element_type=F32)
        obuf[p] = o if j == 0 else obuf[p] + o

    def stage(g_weigh, g_score):
        for j in range(NB):
            if g_score is not None:
                scores(g_score, j)
            if g_weigh is not None:
                weigh(g_weigh, j)
        if g_score is not None:
            p = g_score % 2
            mbuf[2 + p] = jnp.broadcast_to(
                jnp.max(mbuf[p], axis=1, keepdims=True), (TOK, PAIR)
            )

    def finish(g):
        t, p = g // 2, g % 2
        o = obuf[p]
        o = o[:, :PAIR] / o[:, PAIR:]
        abuf[z, t * HALF:(t + 1) * HALF, p * PAIR:(p + 1) * PAIR] = jnp.where(
            low, o[:HALF], o[HALF:]
        ).astype(BF16)

    def a_push(zz, t, dev):
        ref = abuf.at[zz, pl.ds(t * HALF, HALF)]
        send(ref, a_send.at[a_count[0]], a_recv.at[zz * 2 + t], dev)
        a_count[0] += 1

    def a_own(t):
        a_push(z, t, (z_right, tgt))
        a_push(z, t, (z_left, tgt))

    def o_part(zz, t):
        rows = slice(t * HALF, (t + 1) * HALF)
        a = abuf[zz, rows, :]
        w = wo[pl.ds(pl.multiple_of((zz * 2 + yh) * FEAT, FEAT), FEAT), :]
        qacc[rows, :] += jnp.dot(a, w, preferred_element_type=F32)
        pacc[rows, :] += jnp.dot(a, wop[zz], preferred_element_type=F32)

    def a_take(dist, t, way):
        zz = (z - dist + NZ) % NZ if way == "R" else (z + dist) % NZ
        arrived(abuf.at[zz, pl.ds(t * HALF, HALF)], a_recv.at[zz * 2 + t])
        if dist < 3 or (dist == 3 and way == "RL"[t]):
            a_push(zz, t, (z_right if way == "R" else z_left, tgt))
        todo.append((zz, t))
        flush()

    def exchange(t):
        pbuf[t] = pacc[t * HALF:(t + 1) * HALF, :].astype(BF16)
        c = pltpu.make_async_remote_copy(
            src_ref=pbuf.at[t], dst_ref=rbuf.at[t], send_sem=p_send.at[t], recv_sem=p_recv.at[t],
            device_id=(partner, tgt), device_id_type=MESH,
        )
        c.start()
        pending.append(c)

    def attend(n):
        if n == 0:
            drain(0, 0)
            make_queries()
        if n == 1:
            drain(0)
        stage(n - 1 if n else None, n if n < 4 else None)
        if n:
            finish(n - 1)
        if n in (2, 4):
            t = n // 2 - 1
            a_own(t)
            todo.append((z, t))
            flush()

    Z, C, F, Y, X, W = take_z, cross_z, first_row, take_y, take_x, take_far
    O, OY, OX, OF, OE = send_wo, take_wo, take_wo_x, take_wo_far, end_wo
    S, A, E = attend, a_take, exchange
    for event in (
        (Z, 0, 1, 0, "R"), (Z, 0, 1, 0, "L"), (F,), (Y, 1, 0), (X, 0, 0, "r"), (X, 0, 0, "l"),
        (Z, 0, 1, 1, "R"), (X, 0, 1, "l"), (X, 0, 1, "r"), (Z, 0, 1, 1, "L"), (Y, 1, 1), (Z, 0, 2, 0, "R"),
        (Z, 0, 2, 0, "L"), (X, 1, 0, "l"), (X, 1, 0, "r"), (Y, 2, 0), (C, 0), (W, 0, 0), (Z, 0, 2, 1, "R"),
        (C, 1), (Z, 0, 2, 1, "L"), (Y, 2, 1), (X, 1, 1, "l"), (Y, 3, 0), (Z, 0, 3, 0, "R"), (X, 2, 0, "l"),
        (Z, 1, 1, 0, "L"), (X, 1, 1, "r"), (Z, 1, 1, 0, "R"), (W, 0, 1), (X, 2, 0, "r"), (Z, 1, 1, 1, "L"),
        (X, 2, 1, "l"), (Y, 3, 1), (O,), (Z, 1, 1, 1, "R"), (W, 1, 0), (Z, 1, 2, 0, "L"),
        (Z, 0, 3, 1, "R"), (X, 3, 0, "l"), (W, 1, 1), (Z, 1, 2, 0, "R"), (Z, 1, 2, 1, "L"), (W, 2, 1),
        (X, 2, 1, "r"), (Z, 0, 3, 1, "L"), (X, 3, 1, "r"), (Z, 1, 3, 0, "L"), (W, 2, 0), (Z, 1, 2, 1, "R"),
        (X, 3, 1, "l"), (X, 3, 0, "r"), (Z, 1, 3, 1, "L"), (W, 3, 0), (Z, 0, 3, 0, "L"), (Z, 0, 4, 1, "R"),
        (OY, 0), (Z, 0, 4, 0, "R"), (W, 3, 1), (Z, 1, 4, 0, "L"), (Z, 1, 3, 0, "R"), (Z, 1, 3, 1, "R"),
        (OY, 1), (Z, 1, 4, 1, "L"), (S, 0), (S, 1), (OX, 0, "l"), (S, 2), (OX, 1, "r"), (S, 3), (S, 4),
        (OX, 1, "l"), (OX, 0, "r"), (OF, 1), (OF, 0), (A, 1, 0, "R"), (A, 1, 0, "L"), (OE,),
        (A, 1, 1, "L"), (A, 2, 0, "R"), (A, 2, 0, "L"), (A, 1, 1, "R"), (A, 2, 1, "L"), (A, 3, 0, "R"),
        (A, 3, 0, "L"), (A, 2, 1, "R"), (A, 3, 1, "L"), (A, 4, 0, "R"), (E, 0), (A, 3, 1, "R"),
        (A, 4, 1, "L"), (E, 1),
    ):
        event[0](*event[1:])
        drain(LAG)

    for t in range(2):
        arrived(rbuf.at[t], p_recv.at[t])
        rows = slice(t * HALF, (t + 1) * HALF)
        out_ref[rows, :] = qacc[rows, :] + rbuf[t].astype(F32)
    for c in pending:
        c.wait_send()
    for when, c in guarded:
        pl.when(when)(c.wait_send)


def body(hidden_in, norm_gain, w_query, keys_cache, values_cache, lengths, w_output):
    gain = norm_gain.astype(F32).reshape(SRC, 1, FEAT)
    anywhere = pl.BlockSpec(memory_space=pl.ANY)
    vmem = pl.BlockSpec(memory_space=pltpu.VMEM)
    smem = pl.BlockSpec(memory_space=pltpu.SMEM)
    dma = pltpu.SemaphoreType.DMA
    branch = pl.pallas_call(
        kernel,
        out_shape=jax.ShapeDtypeStruct((TOK, FEAT), F32),
        in_specs=[anywhere, vmem, anywhere, anywhere, anywhere, smem, anywhere],
        out_specs=vmem,
        scratch_shapes=[
            pltpu.VMEM((SRC, TOK, FEAT), BF16),
            pltpu.VMEM((TGT, 2, POS, FEAT), BF16),
            pltpu.VMEM((WIDE, FEAT), BF16),
            pltpu.VMEM((2, WIDE, FEAT), BF16),
            pltpu.VMEM((WIDE, FEAT), BF16),
            pltpu.VMEM((WIDE, FEAT), BF16),
            pltpu.VMEM((NZ, FEAT, FEAT), BF16),
            pltpu.VMEM((NZ, TOK, FEAT), BF16),
            pltpu.VMEM((2, NB, TOK, BLK), F32),
            pltpu.VMEM((4, TOK, PAIR), F32),
            pltpu.VMEM((2, TOK, FEAT), F32),
            pltpu.VMEM((TOK, FEAT), F32),
            pltpu.VMEM((TOK, FEAT), F32),
            pltpu.VMEM((2, HALF, FEAT), BF16),
            pltpu.VMEM((2, HALF, FEAT), BF16),
            pltpu.VMEM((TOK, PAIR), F32),
            pltpu.VMEM((4, TOK, PAIR), BF16),
            pltpu.VMEM((8, FEAT), F32),
            dma((5,)),
            dma((32,)), dma((32,)),
            dma((16,)), dma((16,)),
            dma((100,)), dma((64,)), dma((20,)), dma((16,)), dma((2,)), dma((2,)),
        ],
        compiler_params=pltpu.CompilerParams(
            collective_id=0, has_side_effects=True, vmem_limit_bytes=63 * 1024 * 1024,
        ),
        cost_estimate=pl.CostEstimate(
            flops=6_000_000_000, bytes_accessed=8_000_000, transcendentals=4_200_000
        ),
    )(hidden_in, gain, w_query, keys_cache, values_cache, lengths, w_output)
    return hidden_in.astype(F32) + branch


def solution(mesh):
    in_specs = (
        P("tgt", "src"),
        P(),
        P(None, "src"),
        P("tgt", "src"),
        P("tgt", "src"),
        P(),
        P(None, "src"),
    )
    out_specs = P("tgt", "src")
    return jax.shard_map(body, mesh=mesh, in_specs=in_specs, out_specs=out_specs, check_vma=False)
```

```python
import functools

import jax
import jax.numpy as jnp
from jax import lax
from jax.experimental import pallas as pl
from jax.experimental.pallas import tpu as pltpu
from jax.sharding import PartitionSpec as P

MESH = pl.DeviceIdType.MESH
HD = 64
NZ, NX, NYL = 8, 4, 4
SRC, TGT = 16, 32
TOK, FEAT, POS, WIDE = 256, 256, 128, 4096
PAIR = 128
HALF = 128
LAG = 6
BLK = 512
NB = WIDE // BLK
SCALE = HD ** -0.5 * 1.4426950408889634
F32, BF16 = jnp.float32, jnp.bfloat16
NT = (((1,), (1,)), ((), ()))


def kernel(
    hid_hbm, gain_in, wq_hbm, keys_hbm, vals_hbm, len_ref, wo_hbm, out_ref,
    hbuf, kv, kc, vp, wq, wo, wop, abuf, sbuf, mbuf, obuf, qacc, pacc, pbuf, rbuf, ssq, qm, krow, gain_ref,
    loc_sem, h_send, h_recv, a_send, a_recv, kv_send, kv_recv, w_send, w_recv, p_send, p_recv,
):
    src = lax.axis_index("src")
    tgt = lax.axis_index("tgt")
    z, yh = src // 2, src % 2
    x, yl, core = tgt // 8, (tgt // 2) % 4, tgt % 2
    partner = z * 2 + (1 - yh)
    z_right = ((z + 1) % NZ) * 2 + yh
    z_left = ((z + NZ - 1) % NZ) * 2 + yh
    sib = x * 8 + yl * 2 + (1 - core)

    def at_tgt(xx, yy):
        return (xx % NX) * 8 + (yy % NYL) * 2 + core

    x_right, x_left = at_tgt(x + 1, yl), at_tgt(x + NX - 1, yl)
    edge = yl == 0
    rows_from = [
        yl,
        jnp.where(edge, 1, yl - 1),
        jnp.where(edge, 2, jnp.where(yl == 3, 1, yl + 1)),
        jnp.where(yl < 2, 3, 0),
    ]

    loads = [
        pltpu.make_async_copy(hid_hbm, hbuf.at[src], loc_sem.at[0]),
        pltpu.make_async_copy(keys_hbm, kv.at[tgt, 0], loc_sem.at[1]),
        pltpu.make_async_copy(vals_hbm, kv.at[tgt, 1], loc_sem.at[2]),
        pltpu.make_async_copy(wq_hbm, wq, loc_sem.at[3]),
        pltpu.make_async_copy(wo_hbm, wo, loc_sem.at[4]),
    ]
    for c in loads:
        c.start()

    barrier = pltpu.get_barrier_semaphore()
    friends = [
        (partner, tgt), (z_right, tgt), (z_left, tgt),
        (src, x_right), (src, x_left), (src, sib),
        (src, at_tgt(x, yl + 1)), (src, at_tgt(x, yl + NYL - 1)),
    ]
    for f in friends:
        pl.semaphore_signal(barrier, inc=1, device_id=f, device_id_type=MESH)

    for o in range(SRC):
        gain_ref[o] = gain_in[o * FEAT:(o + 1) * FEAT].astype(F32).reshape(1, FEAT)
    qacc[...] = jnp.zeros_like(qacc)
    ssq[...] = jnp.zeros_like(ssq)
    for c in loads[:3]:
        c.wait()
    pl.semaphore_wait(barrier, len(friends))

    pending, guarded = [], []

    def send(ref, ssem, rsem, dev):
        c = pltpu.make_async_remote_copy(
            src_ref=ref, dst_ref=ref, send_sem=ssem, recv_sem=rsem,
            device_id=dev, device_id_type=MESH,
        )
        c.start()
        pending.append(c)

    def arrived(ref, rsem):
        pltpu.make_async_remote_copy(
            src_ref=ref, dst_ref=ref, send_sem=rsem, recv_sem=rsem,
            device_id=(src, sib), device_id_type=MESH,
        ).wait_recv()

    def owner_of(col, dist, way):
        zz = (z - dist + NZ) % NZ if way == "R" else (z + dist) % NZ
        return zz * 2 + (yh if col == 0 else 1 - yh)

    class Ring:
        def __init__(self, slot, ssem, rsem):
            self.slot, self.ssem, self.rsem, self.count = slot, ssem, rsem, 0

        def push(self, owner, half, dev):
            send(self.slot(owner, half), self.ssem.at[self.count], self.rsem.at[owner * 2 + half], dev)
            self.count += 1

        def own(self, half):
            self.push(src, half, (z_right, tgt))
            self.push(src, half, (z_left, tgt))
            self.push(src, half, (partner, tgt))

        def take(self, col, dist, way, half):
            owner = owner_of(col, dist, way)
            arrived(self.slot(owner, half), self.rsem.at[owner * 2 + half])
            last = {("R", 0): 3, ("R", 1): 2, ("L", 0): 2, ("L", 1): 3}[(way, col)]
            if dist <= last:
                self.push(owner, half, (z_right if way == "R" else z_left, tgt))
            return owner

        def cross(self, half):
            arrived(self.slot(partner, half), self.rsem.at[partner * 2 + half])
            self.push(partner, half, (z_right, tgt))
            self.push(partner, half, (z_left, tgt))

    hid = Ring(lambda o, h: hbuf.at[o, pl.ds(h * HALF, HALF)], h_send, h_recv)
    kv_count, a_count, w_count = [0], [0], [0]

    def kv_push(s, u, dev):
        send(kv.at[s, u], kv_send.at[kv_count[0]], kv_recv.at[s * 2 + u], dev)
        kv_count[0] += 1

    def kv_wait(s, u):
        arrived(kv.at[s, u], kv_recv.at[s * 2 + u])

    def q_part(owner):
        h = hbuf[owner].astype(F32)
        sq = h * h
        ssq[...] += sq[:, :PAIR] + sq[:, PAIR:]
        hg = (h * gain_ref[owner]).astype(BF16)
        w = wq[pl.ds(pl.multiple_of(owner * FEAT, FEAT), FEAT), :]
        qacc[...] += jnp.dot(hg, w, preferred_element_type=F32)

    def prep(s, u):
        limit = len_ref[s // 2] - (s % 2) * POS
        ok = lax.broadcasted_iota(jnp.int32, (POS, FEAT), 0) < limit
        at = pl.ds(pl.multiple_of(s * POS, POS), POS)
        data = kv[s, u].astype(F32)
        if u == 0:
            kc[at, :] = jnp.where(ok, data, krow[0:1, :]).astype(BF16)
        else:
            data = jnp.where(ok, data, 0.0).astype(BF16)
            mask = jnp.where(ok[:, :PAIR], 1.0, 0.0).astype(BF16)
            for p in range(2):
                vp[p, at, :PAIR] = data[:, p * PAIR:(p + 1) * PAIR]
                vp[p, at, PAIR:] = mask

    for half in range(2):
        hid.own(half)
    def at_yl(yy):
        return x * 8 + yy * 2 + core

    def maybe(when, s, u, dev):
        i = kv_count[0]
        kv_count[0] += 1
        c = pltpu.make_async_remote_copy(
            src_ref=kv.at[s, u], dst_ref=kv.at[s, u], send_sem=kv_send.at[i],
            recv_sem=kv_recv.at[s * 2 + u], device_id=dev, device_id_type=MESH,
        )
        pl.when(when)(c.start)
        guarded.append((when, c))

    for u in range(2):
        maybe(yl < NYL - 1, tgt, u, (src, at_yl(jnp.minimum(yl + 1, NYL - 1))))
        maybe(yl > 0, tgt, u, (src, at_yl(jnp.maximum(yl - 1, 0))))
        kv_push(tgt, u, (src, x_right))
        kv_push(tgt, u, (src, x_left))
        kv_push(tgt, u, (src, sib))
    inner = (yl > 0) & (yl < NYL - 1)

    loads[3].wait()
    q_part(src)

    backlog = []

    def own_taken(s, u):
        kv_push(s, u, (src, sib))
        prep(s, u)
        backlog.append((s + 1 - 2 * core, u))

    def take_y(k, u):
        s = at_yl(rows_from[k])
        kv_wait(s, u)
        onward = jnp.where(rows_from[k] > yl, yl - 1, yl + 1)
        maybe(inner, s, u, (src, at_yl(jnp.clip(onward, 0, NYL - 1))))
        kv_push(s, u, (src, x_right))
        kv_push(s, u, (src, x_left))
        own_taken(s, u)

    def take_x(k, u, way):
        from_left = way == "l"
        s = at_tgt(x + NX - 1 if from_left else x + 1, rows_from[k])
        kv_wait(s, u)
        far_right = (k in (0, 3)) == (u == 0)
        if from_left and far_right:
            kv_push(s, u, (src, x_right))
        if not from_left and not far_right:
            kv_push(s, u, (src, x_left))
        own_taken(s, u)

    def take_far(k, u):
        s = at_tgt(x + 2, rows_from[k])
        kv_wait(s, u)
        own_taken(s, u)

    def drain(keep, only=None):
        spare = len(backlog) - keep if only is None else len(backlog)
        kept = []
        for i, (s, u) in enumerate(backlog):
            if i < spare and only in (None, u):
                kv_wait(s, u)
                prep(s, u)
            else:
                kept.append((s, u))
        backlog[:] = kept

    def first_row():
        other = tgt + 1 - 2 * core
        kv_wait(other, 0)
        even = kv[x * 8 + yl * 2, 0, 0:16, :].astype(F32)[0:1, :]
        krow[...] = jnp.broadcast_to(even, krow.shape)
        prep(tgt, 0)
        prep(tgt, 1)
        prep(other, 0)
        backlog.append((other, 1))

    halves = {}

    def counted(key, owner):
        halves[key] = halves.get(key, 0) + 1
        if halves[key] == 2:
            q_part(owner)

    def take_z(col, dist, half, way):
        counted((col, dist, way), hid.take(col, dist, way, half))

    def cross_z(half):
        hid.cross(half)
        counted("cross", partner)

    def wo_block(xx):
        return (xx % NX) * 2 + core

    def w_push(j, h, dev, ref=None):
        dst = wop.at[j, pl.ds(h * HALF, HALF)]
        c = pltpu.make_async_remote_copy(
            src_ref=dst if ref is None else ref, dst_ref=dst,
            send_sem=w_send.at[w_count[0]], recv_sem=w_recv.at[j * 2 + h],
            device_id=dev, device_id_type=MESH,
        )
        c.start()
        pending.append(c)
        w_count[0] += 1

    def w_wait(j, h):
        arrived(wop.at[j, pl.ds(h * HALF, HALF)], w_recv.at[j * 2 + h])

    def send_wo():
        j = wo_block(x)
        loads[4].wait()
        for h in range(2):
            row = pl.multiple_of((j * 2 + 1 - yh) * FEAT + h * HALF, HALF)
            w_push(j, h, (partner, tgt), wo.at[pl.ds(row, HALF)])

    def take_wo(h):
        j = wo_block(x)
        w_wait(j, h)
        w_push(j, h, (src, x_right))
        w_push(j, h, (src, x_left))
        w_push(j, h, (src, sib))

    def take_wo_x(h, way):
        j = wo_block(x + NX - 1 if way == "l" else x + 1)
        w_wait(j, h)
        if (h, way) == (0, "l"):
            w_push(j, h, (src, x_right))
        if (h, way) == (1, "r"):
            w_push(j, h, (src, x_left))
        w_push(j, h, (src, sib))

    def take_wo_far(h):
        j = wo_block(x + 2)
        w_wait(j, h)
        w_push(j, h, (src, sib))

    ready, todo = [], []

    def flush():
        while ready and todo:
            o_part(*todo.pop(0))

    def end_wo():
        for xx in range(NX):
            for h in range(2):
                w_wait(xx * 2 + 1 - core, h)
        ready.append(1)
        flush()

    low = lax.broadcasted_iota(jnp.int32, (HALF, PAIR), 1) < HD

    def make_queries():
        mean = jnp.sum(ssq[...], axis=1, keepdims=True) / WIDE
        q = qacc[...] * (lax.rsqrt(mean + 1e-06) * SCALE)
        for t in range(2):
            for p in range(2):
                qp = q[t * HALF:(t + 1) * HALF, p * PAIR:(p + 1) * PAIR]
                qm[2 * t + p, :HALF] = jnp.where(low, qp, 0.0).astype(BF16)
                qm[2 * t + p, HALF:] = jnp.where(low, 0.0, qp).astype(BF16)
        qacc[...] = jnp.zeros_like(qacc)
        pacc[...] = jnp.zeros_like(pacc)

    def scores(g, j):
        p = g % 2
        keys = kc[j * BLK:(j + 1) * BLK, p * PAIR:(p + 1) * PAIR]
        s = lax.dot_general(qm[g], keys, NT, preferred_element_type=F32)
        sbuf[p, j] = s
        m = s[:, :PAIR]
        for i in range(1, BLK // PAIR):
            m = jnp.maximum(m, s[:, i * PAIR:(i + 1) * PAIR])
        mbuf[p] = m if j == 0 else jnp.maximum(mbuf[p], m)

    def weigh(g, j):
        p = g % 2
        top = mbuf[2 + p]
        e = [
            jnp.exp2(sbuf[p, j, :, i * PAIR:(i + 1) * PAIR] - top).astype(BF16)
            for i in range(BLK // PAIR)
        ]
        e = jnp.concatenate(e, axis=1)
        o = jnp.dot(e, vp[p, j * BLK:(j + 1) * BLK, :], preferred_element_type=F32)
        obuf[p] = o if j == 0 else obuf[p] + o

    def stage(g_weigh, g_score):
        for j in range(NB):
            if g_score is not None:
                scores(g_score, j)
            if g_weigh is not None:
                weigh(g_weigh, j)
        if g_score is not None:
            p = g_score % 2
            mbuf[2 + p] = jnp.broadcast_to(
                jnp.max(mbuf[p], axis=1, keepdims=True), (TOK, PAIR)
            )

    def finish(g):
        t, p = g // 2, g % 2
        o = obuf[p]
        o = o[:, :PAIR] / o[:, PAIR:]
        abuf[z, t * HALF:(t + 1) * HALF, p * PAIR:(p + 1) * PAIR] = jnp.where(
            low, o[:HALF], o[HALF:]
        ).astype(BF16)

    def a_push(zz, t, dev):
        ref = abuf.at[zz, pl.ds(t * HALF, HALF)]
        send(ref, a_send.at[a_count[0]], a_recv.at[zz * 2 + t], dev)
        a_count[0] += 1

    def a_own(t):
        a_push(z, t, (z_right, tgt))
        a_push(z, t, (z_left, tgt))

    def o_part(zz, t):
        rows = slice(t * HALF, (t + 1) * HALF)
        a = abuf[zz, rows, :]
        w = wo[pl.ds(pl.multiple_of((zz * 2 + yh) * FEAT, FEAT), FEAT), :]
        qacc[rows, :] += jnp.dot(a, w, preferred_element_type=F32)
        pacc[rows, :] += jnp.dot(a, wop[zz], preferred_element_type=F32)

    def a_take(dist, t, way):
        zz = (z - dist + NZ) % NZ if way == "R" else (z + dist) % NZ
        arrived(abuf.at[zz, pl.ds(t * HALF, HALF)], a_recv.at[zz * 2 + t])
        if dist < 3 or (dist == 3 and way == "RL"[t]):
            a_push(zz, t, (z_right if way == "R" else z_left, tgt))
        todo.append((zz, t))
        flush()

    def exchange(t):
        pbuf[t] = pacc[t * HALF:(t + 1) * HALF, :].astype(BF16)
        c = pltpu.make_async_remote_copy(
            src_ref=pbuf.at[t], dst_ref=rbuf.at[t], send_sem=p_send.at[t], recv_sem=p_recv.at[t],
            device_id=(partner, tgt), device_id_type=MESH,
        )
        c.start()
        pending.append(c)

    def attend(n):
        if n == 0:
            drain(0, 0)
            make_queries()
        if n == 1:
            drain(0)
        stage(n - 1 if n else None, n if n < 4 else None)
        if n:
            finish(n - 1)
        if n in (2, 4):
            t = n // 2 - 1
            a_own(t)
            todo.append((z, t))
            flush()

    Z, C, F, Y, X, W = take_z, cross_z, first_row, take_y, take_x, take_far
    O, OY, OX, OF, OE = send_wo, take_wo, take_wo_x, take_wo_far, end_wo
    S, A, E = attend, a_take, exchange
    for event in (
        (Z, 0, 1, 0, "R"), (Z, 0, 1, 0, "L"), (F,), (Y, 1, 0), (X, 0, 0, "r"), (X, 0, 0, "l"),
        (Z, 0, 1, 1, "R"), (X, 0, 1, "l"), (X, 0, 1, "r"), (Z, 0, 1, 1, "L"), (Y, 1, 1), (Z, 0, 2, 0, "R"),
        (Z, 0, 2, 0, "L"), (X, 1, 0, "l"), (X, 1, 0, "r"), (Y, 2, 0), (C, 0), (W, 0, 0), (Z, 0, 2, 1, "R"),
        (C, 1), (Z, 0, 2, 1, "L"), (Y, 2, 1), (X, 1, 1, "l"), (Y, 3, 0), (Z, 0, 3, 0, "R"), (X, 2, 0, "l"),
        (Z, 1, 1, 0, "L"), (X, 1, 1, "r"), (Z, 1, 1, 0, "R"), (W, 0, 1), (X, 2, 0, "r"), (Z, 1, 1, 1, "L"),
        (X, 2, 1, "l"), (Y, 3, 1), (O,), (Z, 1, 1, 1, "R"), (W, 1, 0), (Z, 1, 2, 0, "L"),
        (Z, 0, 3, 1, "R"), (X, 3, 0, "l"), (W, 1, 1), (Z, 1, 2, 0, "R"), (Z, 1, 2, 1, "L"), (W, 2, 1),
        (X, 2, 1, "r"), (Z, 0, 3, 1, "L"), (X, 3, 1, "r"), (Z, 1, 3, 0, "L"), (W, 2, 0), (Z, 1, 2, 1, "R"),
        (X, 3, 1, "l"), (X, 3, 0, "r"), (Z, 1, 3, 1, "L"), (W, 3, 0), (Z, 0, 3, 0, "L"), (Z, 0, 4, 1, "R"),
        (OY, 0), (Z, 0, 4, 0, "R"), (W, 3, 1), (Z, 1, 4, 0, "L"), (Z, 1, 3, 0, "R"), (Z, 1, 3, 1, "R"),
        (OY, 1), (Z, 1, 4, 1, "L"), (S, 0), (S, 1), (OX, 0, "l"), (S, 2), (OX, 1, "r"), (S, 3), (S, 4),
        (OX, 1, "l"), (OX, 0, "r"), (OF, 1), (OF, 0), (A, 1, 0, "R"), (A, 1, 0, "L"), (OE,),
        (A, 1, 1, "L"), (A, 2, 0, "R"), (A, 2, 0, "L"), (A, 1, 1, "R"), (A, 2, 1, "L"), (A, 3, 0, "R"),
        (A, 3, 0, "L"), (A, 2, 1, "R"), (A, 3, 1, "L"), (A, 4, 0, "R"), (E, 0), (A, 3, 1, "R"),
        (A, 4, 1, "L"), (E, 1),
    ):
        event[0](*event[1:])
        drain(LAG)

    for t in range(2):
        arrived(rbuf.at[t], p_recv.at[t])
        rows = slice(t * HALF, (t + 1) * HALF)
        out_ref[rows, :] = qacc[rows, :] + rbuf[t].astype(F32)
    for c in pending:
        c.wait_send()
    for when, c in guarded:
        pl.when(when)(c.wait_send)


def body(hidden_in, norm_gain, w_query, keys_cache, values_cache, lengths, w_output):
    anywhere = pl.BlockSpec(memory_space=pl.ANY)
    vmem = pl.BlockSpec(memory_space=pltpu.VMEM)
    smem = pl.BlockSpec(memory_space=pltpu.SMEM)
    dma = pltpu.SemaphoreType.DMA
    branch = pl.pallas_call(
        kernel,
        out_shape=jax.ShapeDtypeStruct((TOK, FEAT), F32),
        in_specs=[anywhere, vmem, anywhere, anywhere, anywhere, smem, anywhere],
        out_specs=vmem,
        scratch_shapes=[
            pltpu.VMEM((SRC, TOK, FEAT), BF16),
            pltpu.VMEM((TGT, 2, POS, FEAT), BF16),
            pltpu.VMEM((WIDE, FEAT), BF16),
            pltpu.VMEM((2, WIDE, FEAT), BF16),
            pltpu.VMEM((WIDE, FEAT), BF16),
            pltpu.VMEM((WIDE, FEAT), BF16),
            pltpu.VMEM((NZ, FEAT, FEAT), BF16),
            pltpu.VMEM((NZ, TOK, FEAT), BF16),
            pltpu.VMEM((2, NB, TOK, BLK), F32),
            pltpu.VMEM((4, TOK, PAIR), F32),
            pltpu.VMEM((2, TOK, FEAT), F32),
            pltpu.VMEM((TOK, FEAT), F32),
            pltpu.VMEM((TOK, FEAT), F32),
            pltpu.VMEM((2, HALF, FEAT), BF16),
            pltpu.VMEM((2, HALF, FEAT), BF16),
            pltpu.VMEM((TOK, PAIR), F32),
            pltpu.VMEM((4, TOK, PAIR), BF16),
            pltpu.VMEM((8, FEAT), F32),
            pltpu.VMEM((SRC, 1, FEAT), F32),
            dma((5,)),
            dma((32,)), dma((32,)),
            dma((16,)), dma((16,)),
            dma((100,)), dma((64,)), dma((20,)), dma((16,)), dma((2,)), dma((2,)),
        ],
        compiler_params=pltpu.CompilerParams(
            collective_id=0, has_side_effects=True, vmem_limit_bytes=63 * 1024 * 1024,
        ),
        cost_estimate=pl.CostEstimate(
            flops=6_000_000_000, bytes_accessed=8_000_000, transcendentals=4_200_000
        ),
    )(hidden_in, norm_gain, w_query, keys_cache, values_cache, lengths, w_output)
    return hidden_in.astype(F32) + branch


def solution(mesh):
    in_specs = (
        P("tgt", "src"),
        P(),
        P(None, "src"),
        P("tgt", "src"),
        P("tgt", "src"),
        P(),
        P(None, "src"),
    )
    out_specs = P("tgt", "src")
    return jax.shard_map(body, mesh=mesh, in_specs=in_specs, out_specs=out_specs, check_vma=False)
```

```python
import functools

import jax
import jax.numpy as jnp
from jax import lax
from jax.experimental import pallas as pl
from jax.experimental.pallas import tpu as pltpu
from jax.sharding import PartitionSpec as P

MESH = pl.DeviceIdType.MESH
HD = 64
NZ, NX, NYL = 8, 4, 4
SRC, TGT = 16, 32
TOK, FEAT, POS, WIDE = 256, 256, 128, 4096
PAIR = 128
HALF = 128
LAG = 6
BLK = 512
NB = WIDE // BLK
SCALE = HD ** -0.5 * 1.4426950408889634
F32, BF16 = jnp.float32, jnp.bfloat16
NT = (((1,), (1,)), ((), ()))


def kernel(
    hid_hbm, gain_in, wq_hbm, keys_hbm, vals_hbm, len_ref, wo_hbm, out_ref,
    hbuf, kv, kc, vp, wq, wo, wop, abuf, sbuf, mbuf, obuf, qacc, pacc, pbuf, rbuf, ssq, qm, krow, gain_ref,
    loc_sem, h_send, h_recv, a_send, a_recv, kv_send, kv_recv, w_send, w_recv, p_send, p_recv,
):
    src = lax.axis_index("src")
    tgt = lax.axis_index("tgt")
    z, yh = src // 2, src % 2
    x, yl, core = tgt // 8, (tgt // 2) % 4, tgt % 2
    partner = z * 2 + (1 - yh)
    z_right = ((z + 1) % NZ) * 2 + yh
    z_left = ((z + NZ - 1) % NZ) * 2 + yh
    sib = x * 8 + yl * 2 + (1 - core)

    def at_tgt(xx, yy):
        return (xx % NX) * 8 + (yy % NYL) * 2 + core

    x_right, x_left = at_tgt(x + 1, yl), at_tgt(x + NX - 1, yl)
    edge = yl == 0
    rows_from = [
        yl,
        jnp.where(edge, 1, yl - 1),
        jnp.where(edge, 2, jnp.where(yl == 3, 1, yl + 1)),
        jnp.where(yl < 2, 3, 0),
    ]

    loads = [
        pltpu.make_async_copy(hid_hbm, hbuf.at[src], loc_sem.at[0]),
        pltpu.make_async_copy(keys_hbm, kv.at[tgt, 0], loc_sem.at[1]),
        pltpu.make_async_copy(vals_hbm, kv.at[tgt, 1], loc_sem.at[2]),
        pltpu.make_async_copy(wq_hbm, wq, loc_sem.at[3]),
        pltpu.make_async_copy(wo_hbm, wo, loc_sem.at[4]),
    ]
    for c in loads:
        c.start()

    barrier = pltpu.get_barrier_semaphore()
    friends = [
        (partner, tgt), (z_right, tgt), (z_left, tgt),
        (src, x_right), (src, x_left), (src, sib),
        (src, at_tgt(x, yl + 1)), (src, at_tgt(x, yl + NYL - 1)),
    ]
    for f in friends:
        pl.semaphore_signal(barrier, inc=1, device_id=f, device_id_type=MESH)

    qacc[...] = jnp.zeros_like(qacc)
    ssq[...] = jnp.zeros_like(ssq)
    for c in loads[:3]:
        c.wait()
    pl.semaphore_wait(barrier, len(friends))

    pending, guarded = [], []

    def send(ref, ssem, rsem, dev):
        c = pltpu.make_async_remote_copy(
            src_ref=ref, dst_ref=ref, send_sem=ssem, recv_sem=rsem,
            device_id=dev, device_id_type=MESH,
        )
        c.start()
        pending.append(c)

    def arrived(ref, rsem):
        pltpu.make_async_remote_copy(
            src_ref=ref, dst_ref=ref, send_sem=rsem, recv_sem=rsem,
            device_id=(src, sib), device_id_type=MESH,
        ).wait_recv()

    def owner_of(col, dist, way):
        zz = (z - dist + NZ) % NZ if way == "R" else (z + dist) % NZ
        return zz * 2 + (yh if col == 0 else 1 - yh)

    class Ring:
        def __init__(self, slot, ssem, rsem):
            self.slot, self.ssem, self.rsem, self.count = slot, ssem, rsem, 0

        def push(self, owner, half, dev):
            send(self.slot(owner, half), self.ssem.at[self.count], self.rsem.at[owner * 2 + half], dev)
            self.count += 1

        def own(self, half):
            self.push(src, half, (z_right, tgt))
            self.push(src, half, (z_left, tgt))
            self.push(src, half, (partner, tgt))

        def take(self, col, dist, way, half):
            owner = owner_of(col, dist, way)
            arrived(self.slot(owner, half), self.rsem.at[owner * 2 + half])
            last = {("R", 0): 3, ("R", 1): 2, ("L", 0): 2, ("L", 1): 3}[(way, col)]
            if dist <= last:
                self.push(owner, half, (z_right if way == "R" else z_left, tgt))
            return owner

        def cross(self, half):
            arrived(self.slot(partner, half), self.rsem.at[partner * 2 + half])
            self.push(partner, half, (z_right, tgt))
            self.push(partner, half, (z_left, tgt))

    hid = Ring(lambda o, h: hbuf.at[o, pl.ds(h * HALF, HALF)], h_send, h_recv)
    kv_count, a_count, w_count = [0], [0], [0]

    def kv_push(s, u, dev):
        send(kv.at[s, u], kv_send.at[kv_count[0]], kv_recv.at[s * 2 + u], dev)
        kv_count[0] += 1

    def kv_wait(s, u):
        arrived(kv.at[s, u], kv_recv.at[s * 2 + u])

    def q_part(owner):
        h = hbuf[owner].astype(F32)
        sq = h * h
        ssq[...] += sq[:, :PAIR] + sq[:, PAIR:]
        hg = (h * gain_ref[owner]).astype(BF16)
        w = wq[pl.ds(pl.multiple_of(owner * FEAT, FEAT), FEAT), :]
        qacc[...] += jnp.dot(hg, w, preferred_element_type=F32)

    def prep(s, u):
        limit = len_ref[s // 2] - (s % 2) * POS
        ok = lax.broadcasted_iota(jnp.int32, (POS, FEAT), 0) < limit
        at = pl.ds(pl.multiple_of(s * POS, POS), POS)
        data = kv[s, u].astype(F32)
        if u == 0:
            kc[at, :] = jnp.where(ok, data, krow[0:1, :]).astype(BF16)
        else:
            data = jnp.where(ok, data, 0.0).astype(BF16)
            mask = jnp.where(ok[:, :PAIR], 1.0, 0.0).astype(BF16)
            for p in range(2):
                vp[p, at, :PAIR] = data[:, p * PAIR:(p + 1) * PAIR]
                vp[p, at, PAIR:] = mask

    for half in range(2):
        hid.own(half)
    def at_yl(yy):
        return x * 8 + yy * 2 + core

    def maybe(when, s, u, dev):
        i = kv_count[0]
        kv_count[0] += 1
        c = pltpu.make_async_remote_copy(
            src_ref=kv.at[s, u], dst_ref=kv.at[s, u], send_sem=kv_send.at[i],
            recv_sem=kv_recv.at[s * 2 + u], device_id=dev, device_id_type=MESH,
        )
        pl.when(when)(c.start)
        guarded.append((when, c))

    for u in range(2):
        maybe(yl < NYL - 1, tgt, u, (src, at_yl(jnp.minimum(yl + 1, NYL - 1))))
        maybe(yl > 0, tgt, u, (src, at_yl(jnp.maximum(yl - 1, 0))))
        kv_push(tgt, u, (src, x_right))
        kv_push(tgt, u, (src, x_left))
        kv_push(tgt, u, (src, sib))
    inner = (yl > 0) & (yl < NYL - 1)

    for o in range(SRC):
        gain_ref[o] = gain_in[o * FEAT:(o + 1) * FEAT].astype(F32).reshape(1, FEAT)
    loads[3].wait()
    q_part(src)

    backlog = []

    def own_taken(s, u):
        kv_push(s, u, (src, sib))
        prep(s, u)
        backlog.append((s + 1 - 2 * core, u))

    def take_y(k, u):
        s = at_yl(rows_from[k])
        kv_wait(s, u)
        onward = jnp.where(rows_from[k] > yl, yl - 1, yl + 1)
        maybe(inner, s, u, (src, at_yl(jnp.clip(onward, 0, NYL - 1))))
        kv_push(s, u, (src, x_right))
        kv_push(s, u, (src, x_left))
        own_taken(s, u)

    def take_x(k, u, way):
        from_left = way == "l"
        s = at_tgt(x + NX - 1 if from_left else x + 1, rows_from[k])
        kv_wait(s, u)
        far_right = (k in (0, 3)) == (u == 0)
        if from_left and far_right:
            kv_push(s, u, (src, x_right))
        if not from_left and not far_right:
            kv_push(s, u, (src, x_left))
        own_taken(s, u)

    def take_far(k, u):
        s = at_tgt(x + 2, rows_from[k])
        kv_wait(s, u)
        own_taken(s, u)

    def drain(keep, only=None):
        spare = len(backlog) - keep if only is None else len(backlog)
        kept = []
        for i, (s, u) in enumerate(backlog):
            if i < spare and only in (None, u):
                kv_wait(s, u)
                prep(s, u)
            else:
                kept.append((s, u))
        backlog[:] = kept

    def first_row():
        other = tgt + 1 - 2 * core
        kv_wait(other, 0)
        even = kv[x * 8 + yl * 2, 0, 0:16, :].astype(F32)[0:1, :]
        krow[...] = jnp.broadcast_to(even, krow.shape)
        prep(tgt, 0)
        prep(tgt, 1)
        prep(other, 0)
        backlog.append((other, 1))

    halves = {}

    def counted(key, owner):
        halves[key] = halves.get(key, 0) + 1
        if halves[key] == 2:
            q_part(owner)

    def take_z(col, dist, half, way):
        counted((col, dist, way), hid.take(col, dist, way, half))

    def cross_z(half):
        hid.cross(half)
        counted("cross", partner)

    def wo_block(xx):
        return (xx % NX) * 2 + core

    def w_push(j, h, dev, ref=None):
        dst = wop.at[j, pl.ds(h * HALF, HALF)]
        c = pltpu.make_async_remote_copy(
            src_ref=dst if ref is None else ref, dst_ref=dst,
            send_sem=w_send.at[w_count[0]], recv_sem=w_recv.at[j * 2 + h],
            device_id=dev, device_id_type=MESH,
        )
        c.start()
        pending.append(c)
        w_count[0] += 1

    def w_wait(j, h):
        arrived(wop.at[j, pl.ds(h * HALF, HALF)], w_recv.at[j * 2 + h])

    def send_wo():
        j = wo_block(x)
        loads[4].wait()
        for h in range(2):
            row = pl.multiple_of((j * 2 + 1 - yh) * FEAT + h * HALF, HALF)
            w_push(j, h, (partner, tgt), wo.at[pl.ds(row, HALF)])

    def take_wo(h):
        j = wo_block(x)
        w_wait(j, h)
        w_push(j, h, (src, x_right))
        w_push(j, h, (src, x_left))
        w_push(j, h, (src, sib))

    def take_wo_x(h, way):
        j = wo_block(x + NX - 1 if way == "l" else x + 1)
        w_wait(j, h)
        if (h, way) == (0, "l"):
            w_push(j, h, (src, x_right))
        if (h, way) == (1, "r"):
            w_push(j, h, (src, x_left))
        w_push(j, h, (src, sib))

    def take_wo_far(h):
        j = wo_block(x + 2)
        w_wait(j, h)
        w_push(j, h, (src, sib))

    ready, todo = [], []

    def flush():
        while ready and todo:
            o_part(*todo.pop(0))

    def end_wo():
        for xx in range(NX):
            for h in range(2):
                w_wait(xx * 2 + 1 - core, h)
        ready.append(1)
        flush()

    low = lax.broadcasted_iota(jnp.int32, (HALF, PAIR), 1) < HD

    def make_queries():
        mean = jnp.sum(ssq[...], axis=1, keepdims=True) / WIDE
        q = qacc[...] * (lax.rsqrt(mean + 1e-06) * SCALE)
        for t in range(2):
            for p in range(2):
                qp = q[t * HALF:(t + 1) * HALF, p * PAIR:(p + 1) * PAIR]
                qm[2 * t + p, :HALF] = jnp.where(low, qp, 0.0).astype(BF16)
                qm[2 * t + p, HALF:] = jnp.where(low, 0.0, qp).astype(BF16)
        qacc[...] = jnp.zeros_like(qacc)
        pacc[...] = jnp.zeros_like(pacc)

    def scores(g, j):
        p = g % 2
        keys = kc[j * BLK:(j + 1) * BLK, p * PAIR:(p + 1) * PAIR]
        s = lax.dot_general(qm[g], keys, NT, preferred_element_type=F32)
        sbuf[p, j] = s
        m = s[:, :PAIR]
        for i in range(1, BLK // PAIR):
            m = jnp.maximum(m, s[:, i * PAIR:(i + 1) * PAIR])
        mbuf[p] = m if j == 0 else jnp.maximum(mbuf[p], m)

    def weigh(g, j):
        p = g % 2
        top = mbuf[2 + p]
        e = [
            jnp.exp2(sbuf[p, j, :, i * PAIR:(i + 1) * PAIR] - top).astype(BF16)
            for i in range(BLK // PAIR)
        ]
        e = jnp.concatenate(e, axis=1)
        o = jnp.dot(e, vp[p, j * BLK:(j + 1) * BLK, :], preferred_element_type=F32)
        obuf[p] = o if j == 0 else obuf[p] + o

    def stage(g_weigh, g_score):
        for j in range(NB):
            if g_score is not None:
                scores(g_score, j)
            if g_weigh is not None:
                weigh(g_weigh, j)
        if g_score is not None:
            p = g_score % 2
            mbuf[2 + p] = jnp.broadcast_to(
                jnp.max(mbuf[p], axis=1, keepdims=True), (TOK, PAIR)
            )

    def finish(g):
        t, p = g // 2, g % 2
        o = obuf[p]
        o = o[:, :PAIR] / o[:, PAIR:]
        abuf[z, t * HALF:(t + 1) * HALF, p * PAIR:(p + 1) * PAIR] = jnp.where(
            low, o[:HALF], o[HALF:]
        ).astype(BF16)

    def a_push(zz, t, dev):
        ref = abuf.at[zz, pl.ds(t * HALF, HALF)]
        send(ref, a_send.at[a_count[0]], a_recv.at[zz * 2 + t], dev)
        a_count[0] += 1

    def a_own(t):
        a_push(z, t, (z_right, tgt))
        a_push(z, t, (z_left, tgt))

    def o_part(zz, t):
        rows = slice(t * HALF, (t + 1) * HALF)
        a = abuf[zz, rows, :]
        w = wo[pl.ds(pl.multiple_of((zz * 2 + yh) * FEAT, FEAT), FEAT), :]
        qacc[rows, :] += jnp.dot(a, w, preferred_element_type=F32)
        pacc[rows, :] += jnp.dot(a, wop[zz], preferred_element_type=F32)

    def a_take(dist, t, way):
        zz = (z - dist + NZ) % NZ if way == "R" else (z + dist) % NZ
        arrived(abuf.at[zz, pl.ds(t * HALF, HALF)], a_recv.at[zz * 2 + t])
        if dist < 3 or (dist == 3 and way == "RL"[t]):
            a_push(zz, t, (z_right if way == "R" else z_left, tgt))
        todo.append((zz, t))
        flush()

    def exchange(t):
        pbuf[t] = pacc[t * HALF:(t + 1) * HALF, :].astype(BF16)
        c = pltpu.make_async_remote_copy(
            src_ref=pbuf.at[t], dst_ref=rbuf.at[t], send_sem=p_send.at[t], recv_sem=p_recv.at[t],
            device_id=(partner, tgt), device_id_type=MESH,
        )
        c.start()
        pending.append(c)

    def attend(n):
        if n == 0:
            drain(0, 0)
            make_queries()
        if n == 1:
            drain(0)
        stage(n - 1 if n else None, n if n < 4 else None)
        if n:
            finish(n - 1)
        if n in (2, 4):
            t = n // 2 - 1
            a_own(t)
            todo.append((z, t))
            flush()

    Z, C, F, Y, X, W = take_z, cross_z, first_row, take_y, take_x, take_far
    O, OY, OX, OF, OE = send_wo, take_wo, take_wo_x, take_wo_far, end_wo
    S, A, E = attend, a_take, exchange
    for event in (
        (Z, 0, 1, 0, "R"), (Z, 0, 1, 0, "L"), (F,), (Y, 1, 0), (X, 0, 0, "r"), (X, 0, 0, "l"),
        (Z, 0, 1, 1, "R"), (X, 0, 1, "l"), (X, 0, 1, "r"), (Z, 0, 1, 1, "L"), (Y, 1, 1), (Z, 0, 2, 0, "R"),
        (Z, 0, 2, 0, "L"), (X, 1, 0, "l"), (X, 1, 0, "r"), (Y, 2, 0), (C, 0), (W, 0, 0), (Z, 0, 2, 1, "R"),
        (C, 1), (Z, 0, 2, 1, "L"), (Y, 2, 1), (X, 1, 1, "l"), (Y, 3, 0), (Z, 0, 3, 0, "R"), (X, 2, 0, "l"),
        (Z, 1, 1, 0, "L"), (X, 1, 1, "r"), (Z, 1, 1, 0, "R"), (W, 0, 1), (X, 2, 0, "r"), (Z, 1, 1, 1, "L"),
        (X, 2, 1, "l"), (Y, 3, 1), (O,), (Z, 1, 1, 1, "R"), (W, 1, 0), (Z, 1, 2, 0, "L"),
        (Z, 0, 3, 1, "R"), (X, 3, 0, "l"), (W, 1, 1), (Z, 1, 2, 0, "R"), (Z, 1, 2, 1, "L"), (W, 2, 1),
        (X, 2, 1, "r"), (Z, 0, 3, 1, "L"), (X, 3, 1, "r"), (Z, 1, 3, 0, "L"), (W, 2, 0), (Z, 1, 2, 1, "R"),
        (X, 3, 1, "l"), (X, 3, 0, "r"), (Z, 1, 3, 1, "L"), (W, 3, 0), (Z, 0, 3, 0, "L"), (Z, 0, 4, 1, "R"),
        (OY, 0), (Z, 0, 4, 0, "R"), (W, 3, 1), (Z, 1, 4, 0, "L"), (Z, 1, 3, 0, "R"), (Z, 1, 3, 1, "R"),
        (OY, 1), (Z, 1, 4, 1, "L"), (S, 0), (S, 1), (OX, 0, "l"), (S, 2), (OX, 1, "r"), (S, 3), (S, 4),
        (OX, 1, "l"), (OX, 0, "r"), (OF, 1), (OF, 0), (A, 1, 0, "R"), (A, 1, 0, "L"), (OE,),
        (A, 1, 1, "L"), (A, 2, 0, "R"), (A, 2, 0, "L"), (A, 1, 1, "R"), (A, 2, 1, "L"), (A, 3, 0, "R"),
        (A, 3, 0, "L"), (A, 2, 1, "R"), (A, 3, 1, "L"), (A, 4, 0, "R"), (E, 0), (A, 3, 1, "R"),
        (A, 4, 1, "L"), (E, 1),
    ):
        event[0](*event[1:])
        drain(LAG)

    for t in range(2):
        arrived(rbuf.at[t], p_recv.at[t])
        rows = slice(t * HALF, (t + 1) * HALF)
        out_ref[rows, :] = qacc[rows, :] + rbuf[t].astype(F32)
    for c in pending:
        c.wait_send()
    for when, c in guarded:
        pl.when(when)(c.wait_send)


def body(hidden_in, norm_gain, w_query, keys_cache, values_cache, lengths, w_output):
    anywhere = pl.BlockSpec(memory_space=pl.ANY)
    vmem = pl.BlockSpec(memory_space=pltpu.VMEM)
    smem = pl.BlockSpec(memory_space=pltpu.SMEM)
    dma = pltpu.SemaphoreType.DMA
    branch = pl.pallas_call(
        kernel,
        out_shape=jax.ShapeDtypeStruct((TOK, FEAT), F32),
        in_specs=[anywhere, vmem, anywhere, anywhere, anywhere, smem, anywhere],
        out_specs=vmem,
        scratch_shapes=[
            pltpu.VMEM((SRC, TOK, FEAT), BF16),
            pltpu.VMEM((TGT, 2, POS, FEAT), BF16),
            pltpu.VMEM((WIDE, FEAT), BF16),
            pltpu.VMEM((2, WIDE, FEAT), BF16),
            pltpu.VMEM((WIDE, FEAT), BF16),
            pltpu.VMEM((WIDE, FEAT), BF16),
            pltpu.VMEM((NZ, FEAT, FEAT), BF16),
            pltpu.VMEM((NZ, TOK, FEAT), BF16),
            pltpu.VMEM((2, NB, TOK, BLK), F32),
            pltpu.VMEM((4, TOK, PAIR), F32),
            pltpu.VMEM((2, TOK, FEAT), F32),
            pltpu.VMEM((TOK, FEAT), F32),
            pltpu.VMEM((TOK, FEAT), F32),
            pltpu.VMEM((2, HALF, FEAT), BF16),
            pltpu.VMEM((2, HALF, FEAT), BF16),
            pltpu.VMEM((TOK, PAIR), F32),
            pltpu.VMEM((4, TOK, PAIR), BF16),
            pltpu.VMEM((8, FEAT), F32),
            pltpu.VMEM((SRC, 1, FEAT), F32),
            dma((5,)),
            dma((32,)), dma((32,)),
            dma((16,)), dma((16,)),
            dma((100,)), dma((64,)), dma((20,)), dma((16,)), dma((2,)), dma((2,)),
        ],
        compiler_params=pltpu.CompilerParams(
            collective_id=0, has_side_effects=True, vmem_limit_bytes=63 * 1024 * 1024,
        ),
        cost_estimate=pl.CostEstimate(
            flops=6_000_000_000, bytes_accessed=8_000_000, transcendentals=4_200_000
        ),
    )(hidden_in, norm_gain, w_query, keys_cache, values_cache, lengths, w_output)
    return hidden_in.astype(F32) + branch


def solution(mesh):
    in_specs = (
        P("tgt", "src"),
        P(),
        P(None, "src"),
        P("tgt", "src"),
        P("tgt", "src"),
        P(),
        P(None, "src"),
    )
    out_specs = P("tgt", "src")
    return jax.shard_map(body, mesh=mesh, in_specs=in_specs, out_specs=out_specs, check_vma=False)
```
